256 devices in a mesh: blk: 8 (over z), col: 32 (over y, x, core).
Axes of the slice: x: 4, y: 4, z: 8, core: 2. Of those that a mesh axis runs over, the one named last changes fastest.
Arguments:
- loads: bfloat16 [65536, 256], P('col'), may hold values from -6 to 6
- dense_blocks: bfloat16 [8, 32, 60, 256, 256], P('blk', 'col'), may hold values from -0.046875 to 0.046875
- dense_source: int32 [8, 32, 60], P('blk', 'col'), may hold values from 0 to 7
- dense_target: int32 [8, 32, 60], P('blk', 'col'), may hold values from 0 to 31
- left_factors: bfloat16 [8, 32, 64, 32, 256], P('blk', 'col'), may hold values from -0.375 to 0.375
- right_factors: bfloat16 [8, 32, 64, 32, 256], P('blk', 'col'), may hold values from -0.125 to 0.125
- block_owner: int32 [8, 32, 64, 1], P(None, 'col'), may hold values from 0 to 7; in each aligned block of 64 rows (0 to 63, 64 to 127, ..., all dimensions but the last counted through in order) at most 16 rows name the same one
- block_source: int32 [8, 32, 64], P(None, 'col'), may hold values from 0 to 7
- block_target: int32 [8, 32, 64], P(None, 'col'), may hold values from 0 to 31
Outputs:
- adjoint: bfloat16 [65536, 256], P(('blk', 'col'))
The draws below stay inside these ranges and needn't reach their ends.
Inputs may be any that keep to these rules, and one draw needn't show every extreme that they name: `block_owner`: among the 64 blocks stored on one device no owner is named more than 16 times.
All inputs are finite; a program needn't handle non-finite values.
Results may differ from the reference program's by a relative error of at most 0.0039.
Values may be sent and summed in bfloat16 or wider, within the bound.
A program may use at most 128 MiB of HBM per device.

```python
import math
import jax
import jax.numpy as jnp
import numpy as np
from jax import lax

LEAF = 256
RANK = 32
CASES = 256
SC_DEV = 8
TC_PER = 1
ND_DEV = 60
LR_DEV = 64
CAP = 16
TC = 32
SRC_ROWS = 65536
N_BLK = 8
N_COL = 32


def touch_ends(result, own_key, least, largest):
    spot = [jax.random.randint(jax.random.fold_in(own_key, axis), (), 0, length) for axis, length in enumerate(result.shape)]
    widest = result.shape.index(max(result.shape))
    beside = spot[:widest] + [(spot[widest] + 1) % result.shape[widest]] + spot[widest + 1:]
    return result.at[tuple(spot)].set(least).at[tuple(beside)].set(largest)


def shard_levels(rng, shape, shards, low, top_value):
    factor_of, own = 1.0, jax.random.fold_in(rng, 6)
    for position, blocks in shards:
        steps = jnp.exp(jax.random.uniform(jax.random.fold_in(own, position), (blocks,), jnp.float32, low / len(shards), top_value / len(shards)))
        factor_of = factor_of * jnp.repeat(steps, shape[position] // blocks).reshape([-1 if axis == position else 1 for axis in range(len(shape))])
    return factor_of


def assign_block(own_key, own, number, rows, count, top, bound, lean):
    ranking = jax.random.permutation(own_key, count)
    heavy_load, common = load_shares(count, rows * top, bound, lean, True), load_shares(count, rows * top, bound, lean, False)
    places = jnp.arange(count)

    def named(tallies, offset_by):
        used = int((tallies > 0).sum())
        fixed = max(1, used // 4)
        passed = fixed + (places - fixed + offset_by * (used - fixed)) % max(1, count - fixed)
        return jnp.zeros((count,), jnp.int32).at[ranking[jnp.where(places < fixed, places, passed)]].set(jnp.asarray(tallies, jnp.int32))

    tallies = jnp.where(number % 4 == 0, named(heavy_load, number // 4), named(common, number - number // 4 - 1))
    mixed = jax.random.permutation(jax.random.fold_in(own, 3), count)
    giver, receiver = mixed[0:count // 2 * 2:2], mixed[1:count // 2 * 2:2]
    slack = jnp.minimum(tallies[giver] - 1, bound - tallies[receiver]) // 2
    slack = jnp.where((giver == ranking[0]) | (receiver == ranking[0]) | (tallies[receiver] == 0), 0, jnp.maximum(slack, 0))
    passed = jax.random.randint(jax.random.fold_in(own, 4), (count // 2,), 0, 1 << 20) % (slack + 1)
    tallies = tallies.at[giver].add(-passed).at[receiver].add(passed)
    members = jnp.searchsorted(jnp.cumsum(tallies), jnp.arange(rows * top), side="right").astype(jnp.int32)
    listing = members.reshape(top, rows).T
    listing = listing[jax.random.permutation(jax.random.fold_in(own, 1), rows)]
    offset_by = jax.random.randint(jax.random.fold_in(own, 2), (rows, 1), 0, top)
    return jnp.take_along_axis(listing, (jnp.arange(top)[None, :] + offset_by) % top, axis=1)


def load_shares(amount, total, limit, skew, full):
    portions = [(1 << 20) // math.isqrt(rank ** skew) + 1 for rank in range(1, amount + 1)]
    largest = limit if full else min(limit, max(-(-total // amount), total * portions[0] // sum(portions)))
    least = 1 if total - largest >= amount - 1 else 0
    holding, surplus = [largest] + [least] * (amount - 1), total - largest - least * (amount - 1)
    while surplus > 0:
        candidates = [i for i in range(1, amount) if holding[i] < largest] or [i for i in range(1, amount) if holding[i] < limit]
        pool, remaining = sum([portions[i] for i in candidates]), surplus
        for i in candidates:
            more = min(limit - holding[i], max(1, remaining * portions[i] // pool), surplus)
            holding[i] = holding[i] + more
            surplus = surplus - more
    return np.array(holding)


def normal_values(stream_key, shape, width, most, shards=(), kind=jnp.bfloat16):
    result = jax.random.normal(stream_key, shape, jnp.float32) * width
    if len(shards) > 0:
        result = shard_levels(stream_key, shape, shards, -0.22, 0.18) * result
    return jnp.clip(result, min=-most, max=most).astype(kind)


def setup_inputs(seed: int = 0) -> dict:
    arg_keys = jax.random.split(jax.random.key(seed), 10)
    loads = normal_values(arg_keys[0], (SRC_ROWS, CASES), 1.0, 6.0, ((0, 32),))
    dense_blocks = normal_values(arg_keys[1], (N_BLK, N_COL, ND_DEV, LEAF, LEAF), (LEAF * ND_DEV // TC_PER) ** -0.5, 0.046875, ((0, 8), (1, 32)))
    dense_source = touch_ends(jax.random.randint(arg_keys[2], (N_BLK, N_COL, ND_DEV), 0, SC_DEV), jax.random.fold_in(arg_keys[2], 1), 0, SC_DEV - 1).astype(jnp.int32)
    dense_target = touch_ends(jax.random.randint(arg_keys[3], (N_BLK, N_COL, ND_DEV), 0, TC), jax.random.fold_in(arg_keys[3], 1), 0, TC - 1).astype(jnp.int32)
    left_factors = normal_values(arg_keys[4], (N_BLK, N_COL, LR_DEV, RANK, LEAF), LEAF ** -0.5, 0.375, ((0, 8), (1, 32)))
    right_factors = normal_values(arg_keys[5], (N_BLK, N_COL, LR_DEV, RANK, LEAF), (RANK * LR_DEV // TC_PER) ** -0.5, 0.125, ((0, 8), (1, 32)))
    block_owner_keys = jax.random.split(jax.random.fold_in(arg_keys[6], 1), N_BLK * N_COL * LR_DEV // LR_DEV)
    block_owner_turns = jax.random.permutation(jax.random.fold_in(arg_keys[6], 3), N_BLK * N_COL * LR_DEV // LR_DEV)
    block_owner = jax.vmap(lambda own, number: assign_block(jax.random.fold_in(arg_keys[6], 2), own, number, LR_DEV, N_BLK, 1, CAP, 2))(block_owner_keys, block_owner_turns).reshape((N_BLK, N_COL, LR_DEV, 1))
    block_source = touch_ends(jax.random.randint(arg_keys[7], (N_BLK, N_COL, LR_DEV), 0, SC_DEV), jax.random.fold_in(arg_keys[7], 1), 0, SC_DEV - 1).astype(jnp.int32)
    block_target = touch_ends(jax.random.randint(arg_keys[8], (N_BLK, N_COL, LR_DEV), 0, TC), jax.random.fold_in(arg_keys[8], 1), 0, TC - 1).astype(jnp.int32)
    return {"loads": loads, "dense_blocks": dense_blocks, "dense_source": dense_source, "dense_target": dense_target, "left_factors": left_factors, "right_factors": right_factors, "block_owner": block_owner, "block_source": block_source, "block_target": block_target}


def reference(loads, dense_blocks, dense_source, dense_target, left_factors, right_factors, block_owner, block_source, block_target):
    clusters = TC_PER * N_COL
    devices = N_BLK * N_COL
    grouped = loads.reshape(N_COL, SC_DEV, LEAF, CASES)
    order = jnp.arange(devices, dtype=jnp.int32)
    accumulated = jnp.zeros((N_BLK * clusters, LEAF, CASES), jnp.float32)

    def dense_step(accumulated, current):
        panels, source_ids, target_ids, device = current
        column = device % N_COL
        row_group = device // N_COL
        source_group = lax.dynamic_index_in_dim(grouped, column, 0, keepdims=False)
        picked = source_group[source_ids].astype(jnp.float32)
        contributions = jnp.einsum("nij,nir->njr", panels.astype(jnp.float32), picked)
        return accumulated.at[row_group * clusters + target_ids].add(contributions), None

    accumulated, unused = lax.scan(dense_step, accumulated, (
        dense_blocks.reshape(devices, ND_DEV, LEAF, LEAF),
        dense_source.reshape(devices, ND_DEV),
        dense_target.reshape(devices, ND_DEV),
        order))

    def rank_step(accumulated, current):
        left_panels, right_panels, owners, source_ids, target_ids, device = current
        column = device % N_COL
        source_group = lax.dynamic_index_in_dim(grouped, column, 0, keepdims=False)
        picked = source_group[source_ids].astype(jnp.float32)
        coefficients = jnp.einsum("nki,nir->nkr", left_panels.astype(jnp.float32), picked).astype(jnp.bfloat16)
        coefficients = lax.optimization_barrier(coefficients).astype(jnp.float32)
        contributions = jnp.einsum("nki,nkr->nir", right_panels.astype(jnp.float32), coefficients)
        return accumulated.at[owners * clusters + target_ids].add(contributions), None

    accumulated, unused = lax.scan(rank_step, accumulated, (
        left_factors.reshape(devices, LR_DEV, RANK, LEAF),
        right_factors.reshape(devices, LR_DEV, RANK, LEAF),
        block_owner.reshape(devices, LR_DEV),
        block_source.reshape(devices, LR_DEV),
        block_target.reshape(devices, LR_DEV),
        order))
    return accumulated.reshape(N_BLK * clusters * LEAF, CASES).astype(jnp.bfloat16)
```

```python
import jax
import jax.numpy as jnp
from jax import lax
from jax.experimental import pallas as pl
from jax.experimental.pallas import tpu as pltpu
from jax.sharding import PartitionSpec as P

LEAF = 256
HALF = 128
CASES = 256
RANK = 32
SOURCES = 8
TARGETS = 32
DENSE = 60
LOW = 64
CAP = 16
PLANES = 8
NEAR = (1, 7, 2, 6)
FAR = (4, 3, 5)
MESH = pl.DeviceIdType.MESH
MIB = 1 << 20
BF16 = jnp.bfloat16
F32 = jnp.float32


def spec(space):
    return pl.BlockSpec(memory_space=space)


def place():
    b = lax.axis_index("blk")
    c = lax.axis_index("col")
    return b, lax.div(c, 8), lax.rem(lax.div(c, 2), 4), lax.rem(c, 2)


def contribution(pair):
    return lax.dot_general(
        pair[RANK:], pair[:RANK], (((0,), (0,)), ((), ())), preferred_element_type=F32
    )


def pack_kernel(
    owner, source, target, loads, left, right, slots, far, acc, stage, zero, count, where, seen, sem
):
    b = lax.axis_index("blk")
    zero[...] = jnp.zeros_like(zero)
    for d in range(PLANES):
        count[d] = 0

    @pl.loop(0, len(FAR) * TARGETS)
    def _(i):
        seen[i] = 0

    def one(n, carry):
        d = lax.rem(owner[b, n] - b + PLANES, PLANES)
        r = count[d]
        count[d] = r + 1
        where[d * CAP + r] = target[b, n]
        coefficients = jnp.dot(left[n], loads[source[b, n]], preferred_element_type=F32)
        slots[d, r, :RANK, :] = right[n]
        slots[d, r, RANK:, :] = coefficients.astype(BF16)
        return carry

    lax.fori_loop(0, LOW, one, 0, unroll=8)

    for e, d in enumerate(FAR):

        @pl.loop(0, count[d])
        def _(r):
            t = where[d * CAP + r]
            term = contribution(slots[d, r])
            first = seen[e * TARGETS + t] == 0

            @pl.when(first)
            def _():
                acc[t] = term
                seen[e * TARGETS + t] = 1

            @pl.when(jnp.logical_not(first))
            def _():
                acc[t] += term

        @pl.loop(0, TARGETS)
        def _(t):
            has = seen[e * TARGETS + t] == 1

            @pl.when(has)
            def _():
                stage[e, t] = acc[t].astype(BF16)
                pltpu.make_async_copy(stage.at[e, t], far.at[e, t], sem.at[e]).start()

            @pl.when(jnp.logical_not(has))
            def _():
                pltpu.make_async_copy(zero, far.at[e, t], sem.at[e]).start()

    for e in range(len(FAR)):
        pltpu.make_async_copy(stage.at[e], far.at[e], sem.at[e]).wait()


def pack(owner, source, target, loads, left, right):
    return pl.pallas_call(
        pack_kernel,
        out_shape=(
            jax.ShapeDtypeStruct((PLANES, CAP, 2 * RANK, LEAF), BF16),
            jax.ShapeDtypeStruct((len(FAR), TARGETS, CASES, LEAF), BF16),
        ),
        in_specs=[spec(pltpu.SMEM)] * 3 + [spec(pltpu.VMEM)] * 3,
        out_specs=(spec(pltpu.VMEM), spec(pl.ANY)),
        scratch_shapes=[
            pltpu.VMEM((TARGETS, CASES, LEAF), F32),
            pltpu.VMEM((len(FAR), TARGETS, CASES, LEAF), BF16),
            pltpu.VMEM((CASES, LEAF), BF16),
            pltpu.SMEM((PLANES,), jnp.int32),
            pltpu.SMEM((PLANES * CAP,), jnp.int32),
            pltpu.SMEM((len(FAR) * TARGETS,), jnp.int32),
            pltpu.SemaphoreType.DMA((len(FAR),)),
        ],
        compiler_params=pltpu.CompilerParams(vmem_limit_bytes=48 * MIB),
        name="pack",
    )(owner, source, target, loads, left, right)


def reduce_scratch(dtype):
    return [
        pltpu.VMEM((2, 4, 4, HALF, LEAF), dtype),
        pltpu.VMEM((2, 4, 4, HALF, LEAF), dtype),
        pltpu.VMEM((2, 3, 4, HALF, LEAF), BF16),
        pltpu.VMEM((2, 3, 4, HALF, LEAF), BF16),
        pltpu.VMEM((2, 3, HALF, LEAF), BF16),
        pltpu.VMEM((2, 3, HALF, LEAF), BF16),
        pltpu.VMEM((2, HALF, LEAF), F32),
        pltpu.SemaphoreType.DMA((2, 4, 3)),
        pltpu.SemaphoreType.DMA((2, 3, 4)),
    ]


ORDER = (2, 1, 3, 0)


class PlaneSum:
    def __init__(self, source, scratch):
        self.source = source
        (self.own, self.pair, self.s1, self.r1, self.s2, self.r2, self.kept, self.csem, self.nsem) = scratch
        self.b, self.y, self.x, self.k = place()
        self.sends = []

    def device(self, ax, d):
        y, x = self.y, self.x
        if ax == 0:
            x = lax.rem(x + d, 4)
        else:
            y = lax.rem(y + d, 4)
        return (self.b, (y * 4 + x) * 2 + self.k)

    def chunk(self, ax, d, core):
        if ax == 0:
            return self.source.at[:, lax.rem(self.x + d, 4), core, pl.ds(0, HALF), :]
        return self.source.at[lax.rem(self.y + d, 4), :, core, pl.ds(HALF, HALF), :]

    def local_copy(self, ax, d):
        return pltpu.make_async_copy(self.chunk(ax, d, self.k), self.own.at[ax, d], self.csem.at[ax, d, 0])

    def pair_copy(self, ax, d):
        return pltpu.make_async_remote_copy(
            src_ref=self.chunk(ax, d, 1 - self.k),
            dst_ref=self.pair.at[ax, d],
            send_sem=self.csem.at[ax, d, 1],
            recv_sem=self.csem.at[ax, d, 2],
            device_id=(self.b, (self.y * 4 + self.x) * 2 + 1 - self.k),
            device_id_type=MESH,
        )

    def begin(self):
        for d in ORDER:
            for ax in range(2):
                self.pair_copy(ax, d).start()
                self.local_copy(ax, d).start()

    def copy1(self, ax, d):
        return pltpu.make_async_remote_copy(
            src_ref=self.s1.at[ax, d - 1],
            dst_ref=self.r1.at[ax, d - 1],
            send_sem=self.nsem.at[ax, d - 1, 0],
            recv_sem=self.nsem.at[ax, d - 1, 1],
            device_id=self.device(ax, d),
            device_id_type=MESH,
        )

    def copy2(self, ax, d):
        return pltpu.make_async_remote_copy(
            src_ref=self.s2.at[ax, d - 1],
            dst_ref=self.r2.at[ax, d - 1],
            send_sem=self.nsem.at[ax, d - 1, 2],
            recv_sem=self.nsem.at[ax, d - 1, 3],
            device_id=self.device(1 - ax, d),
            device_id_type=MESH,
        )

    def arrived(self, ax, d):
        self.local_copy(ax, d).wait()
        self.pair_copy(ax, d).wait()

    def first(self):
        for d in ORDER[:3]:
            for ax in range(2):
                self.arrived(ax, d)

                @pl.loop(0, 4)
                def _(q):
                    total = self.own[ax, d, q].astype(F32) + self.pair[ax, d, q].astype(F32)
                    self.s1[ax, d - 1, q] = total.astype(BF16)

                self.copy1(ax, d).start()

    def second(self):
        for ax in range(2):
            self.arrived(ax, 0)
            for d in (1, 3, 2):
                self.copy1(ax, d).wait_recv()
            mine = self.y if ax == 0 else self.x
            for d in ORDER:
                q = lax.rem(mine + d, 4)
                total = self.own[ax, 0, q].astype(F32) + self.pair[ax, 0, q].astype(F32)
                for p in range(3):
                    total = total + self.r1[ax, p, q].astype(F32)
                if d == 0:
                    self.kept[ax] = total
                else:
                    self.s2[ax, d - 1] = total.astype(BF16)
                    self.copy2(ax, d).start()

    def total(self, ax):
        for d in (1, 3, 2):
            self.copy2(ax, d).wait_recv()
        total = self.kept[ax]
        for p in range(3):
            total = total + self.r2[ax, p].astype(F32)
        return total

    def finish(self):
        for ax in range(2):
            for d in range(1, 4):
                self.copy1(ax, d).wait_send()
                self.copy2(ax, d).wait_send()

    def partners(self):
        near = [self.device(ax, d) for ax in range(2) for d in range(1, 4)]
        return near + [(self.b, (self.y * 4 + self.x) * 2 + 1 - self.k)]


def greet(partners):
    barrier = pltpu.get_barrier_semaphore()
    for partner in partners:
        pl.semaphore_signal(barrier, inc=1, device_id=partner, device_id_type=MESH)
    pl.semaphore_wait(barrier, len(partners))


def exchange_kernel(slots, far, received, results, *scratch):
    sums = [PlaneSum(far.at[e], scratch[9 * e : 9 * e + 9]) for e in range(len(FAR))]
    zsem = scratch[-1]
    b = lax.axis_index("blk")
    c = lax.axis_index("col")

    def above(d):
        return (lax.rem(b + d, PLANES), c)

    greet(sums[0].partners() + [above(d) for d in NEAR])
    moves = [
        pltpu.make_async_remote_copy(
            src_ref=slots.at[d],
            dst_ref=received.at[i],
            send_sem=zsem.at[i, 0],
            recv_sem=zsem.at[i, 1],
            device_id=above(d),
            device_id_type=MESH,
        )
        for i, d in enumerate(NEAR)
    ]
    for move in moves:
        move.start()
    for s in sums:
        s.begin()
    sums[0].first()
    sums[1].first()
    sums[0].second()
    sums[2].first()
    sums[1].second()
    for e, s in enumerate(sums):
        if e == 2:
            s.second()
        for ax in range(2):
            results[e, ax * HALF : (ax + 1) * HALF, :] = s.total(ax).astype(BF16)
    for s in sums:
        s.finish()
    for move in moves:
        move.wait()


def exchange(slots, far):
    scratch = []
    for _ in FAR:
        scratch += reduce_scratch(BF16)
    return pl.pallas_call(
        exchange_kernel,
        out_shape=(
            jax.ShapeDtypeStruct((len(NEAR), CAP, 2 * RANK, LEAF), BF16),
            jax.ShapeDtypeStruct((len(FAR), CASES, LEAF), BF16),
        ),
        in_specs=[spec(pl.ANY)] * 2,
        out_specs=(spec(pl.ANY), spec(pltpu.VMEM)),
        scratch_shapes=scratch + [pltpu.SemaphoreType.DMA((len(NEAR), 2))],
        compiler_params=pltpu.CompilerParams(
            collective_id=1, has_side_effects=True, vmem_limit_bytes=48 * MIB
        ),
        name="exchange",
    )(slots, far)


def gather_kernel(
    owner, target, dsource, dtarget, loads, slots, received, dense, out,
    acc, turned, blocks, pairs, ids, spots, dsem, psem, osem,
):
    b = lax.axis_index("blk")
    pieces = 4
    part = DENSE // pieces
    pair_copies = [
        pltpu.make_async_copy(slots.at[0], pairs.at[pl.ds(0, CAP)], psem.at[0])
    ] + [
        pltpu.make_async_copy(received.at[i], pairs.at[pl.ds((i + 1) * CAP, CAP)], psem.at[i + 1])
        for i in range(len(NEAR))
    ]
    dense_copies = [
        pltpu.make_async_copy(dense.at[pl.ds(p * part, part)], blocks.at[pl.ds(p * part, part)], dsem.at[p])
        for p in range(pieces)
    ]
    for copy in pair_copies + dense_copies:
        copy.start()

    @pl.loop(0, TARGETS)
    def _(t):
        acc[t] = jnp.zeros((CASES, LEAF), F32)

    for s in range(SOURCES):
        turned[s] = loads[s].T

    length = jnp.int32(0)
    for i, d in enumerate((0,) + NEAR):
        sender = lax.rem(b - d + PLANES, PLANES)

        def scan(n, carry, i=i, sender=sender):
            length, rank = carry
            hit = owner[sender, n] == b
            ids[length] = target[sender, n]
            spots[length] = i * CAP + rank
            step = hit.astype(jnp.int32)
            return length + step, rank + step

        length, _ = lax.fori_loop(0, LOW, scan, (length, jnp.int32(0)), unroll=8)

    for copy in pair_copies:
        copy.wait()

    @pl.loop(0, length)
    def _(j):
        acc[ids[j]] += contribution(pairs[spots[j]])

    for p in range(pieces):
        dense_copies[p].wait()

        @pl.loop(p * part, (p + 1) * part)
        def _(n):
            acc[dtarget[n]] += jnp.dot(turned[dsource[n]], blocks[n], preferred_element_type=F32)

    whole = pltpu.make_async_copy(acc, out, osem)
    whole.start()
    whole.wait()


def gather(owner, target, dsource, dtarget, loads, slots, received, dense):
    return pl.pallas_call(
        gather_kernel,
        out_shape=jax.ShapeDtypeStruct((TARGETS, CASES, LEAF), F32),
        in_specs=[spec(pltpu.SMEM)] * 4 + [spec(pltpu.VMEM)] + [spec(pl.ANY)] * 3,
        out_specs=spec(pl.ANY),
        scratch_shapes=[
            pltpu.VMEM((TARGETS, CASES, LEAF), F32),
            pltpu.VMEM((SOURCES, CASES, LEAF), BF16),
            pltpu.VMEM((DENSE, LEAF, LEAF), BF16),
            pltpu.VMEM(((1 + len(NEAR)) * CAP, 2 * RANK, LEAF), BF16),
            pltpu.SMEM(((1 + len(NEAR)) * CAP + 1,), jnp.int32),
            pltpu.SMEM(((1 + len(NEAR)) * CAP + 1,), jnp.int32),
            pltpu.SemaphoreType.DMA((4,)),
            pltpu.SemaphoreType.DMA((1 + len(NEAR),)),
            pltpu.SemaphoreType.DMA,
        ],
        compiler_params=pltpu.CompilerParams(vmem_limit_bytes=48 * MIB),
        name="gather",
    )(owner, target, dsource, dtarget, loads, slots, received, dense)


def final_kernel(source, results, out, *scratch):
    own = PlaneSum(source, scratch[:9])
    landed, zsem = scratch[9:]
    b = lax.axis_index("blk")
    c = lax.axis_index("col")

    def above(d):
        return (lax.rem(b + d, PLANES), c)

    greet(own.partners() + [above(d) for d in FAR])
    moves = [
        pltpu.make_async_remote_copy(
            src_ref=results.at[e],
            dst_ref=landed.at[e],
            send_sem=zsem.at[e, 0],
            recv_sem=zsem.at[e, 1],
            device_id=above(d),
            device_id_type=MESH,
        )
        for e, d in enumerate(FAR)
    ]
    own.begin()
    for move in moves:
        move.start()
    own.first()
    own.second()
    for move in moves:
        move.wait()
    for ax in range(2):
        total = own.total(ax)
        for e in range(len(FAR)):
            total = total + landed[e, ax * HALF : (ax + 1) * HALF, :].astype(F32)
        out[:, ax * HALF : (ax + 1) * HALF] = total.T.astype(BF16)
    own.finish()


def final(source, results):
    return pl.pallas_call(
        final_kernel,
        out_shape=jax.ShapeDtypeStruct((LEAF, CASES), BF16),
        in_specs=[spec(pl.ANY)] * 2,
        out_specs=spec(pltpu.VMEM),
        scratch_shapes=reduce_scratch(F32)
        + [pltpu.VMEM((len(FAR), CASES, LEAF), BF16), pltpu.SemaphoreType.DMA((len(FAR), 2))],
        compiler_params=pltpu.CompilerParams(
            collective_id=2, has_side_effects=True, vmem_limit_bytes=48 * MIB
        ),
        name="final",
    )(source, results)


def shards(
    loads,
    dense_blocks,
    dense_source,
    dense_target,
    left_factors,
    right_factors,
    block_owner,
    block_source,
    block_target,
):
    loads = loads.reshape(SOURCES, LEAF, CASES)
    owner = block_owner.reshape(PLANES, LOW)
    source = block_source.reshape(PLANES, LOW)
    target = block_target.reshape(PLANES, LOW)
    left = left_factors.reshape(LOW, RANK, LEAF)
    right = right_factors.reshape(LOW, RANK, LEAF)
    slots, far = pack(owner, source, target, loads, left, right)
    received, results = exchange(slots, far.reshape(len(FAR), 4, 4, 2, CASES, LEAF))
    sums = gather(
        owner, target, dense_source.reshape(DENSE), dense_target.reshape(DENSE),
        loads, slots, received, dense_blocks.reshape(DENSE, LEAF, LEAF),
    )
    return final(sums.reshape(4, 4, 2, CASES, LEAF), results)


def solution(mesh):
    placed = (
        P("col", None),
        P("blk", "col", None, None, None),
        P("blk", "col", None),
        P("blk", "col", None),
        P("blk", "col", None, None, None),
        P("blk", "col", None, None, None),
        P(None, "col", None, None),
        P(None, "col", None),
        P(None, "col", None),
    )
    return jax.shard_map(
        shards, mesh=mesh, in_specs=placed, out_specs=P(("blk", "col"), None), check_vma=False
    )
```

```python
import jax
import jax.numpy as jnp
from jax import lax
from jax.experimental import pallas as pl
from jax.experimental.pallas import tpu as pltpu
from jax.sharding import PartitionSpec as P

LEAF = 256
HALF = 128
CASES = 256
RANK = 32
SOURCES = 8
TARGETS = 32
DENSE = 60
LOW = 64
CAP = 16
PLANES = 8
GROUP = 4
PIECES = 4
ORDERED = 0
SOURCED = 64
TARGETED = 128
SAME = 192
LAST = 256
HAS = 288
IDS = 320
SPOTS = 416
LENGTH = 508
TABLE = 512
NULL = 80
NEAR = (1, 7, 2, 6)
FAR = (4, 3, 5)
MESH = pl.DeviceIdType.MESH
MIB = 1 << 20
BF16 = jnp.bfloat16
F32 = jnp.float32


def spec(space):
    return pl.BlockSpec(memory_space=space)


def place():
    b = lax.axis_index("blk")
    c = lax.axis_index("col")
    return b, lax.div(c, 8), lax.rem(lax.div(c, 2), 4), lax.rem(c, 2)


def contribution(pair):
    return lax.dot_general(
        pair[RANK:], pair[:RANK], (((0,), (0,)), ((), ())), preferred_element_type=F32
    )


def pack_kernel(
    owner_in, source_in, target_in, dsource_in, dtarget_in, loads_in, left_in, right_in, slots_out, far, tables,
    owner, source, target, dsource, dtarget, loads, left, right, slots, acc, stage, zero, count, where, seen,
    tsem, vsem, sem,
):
    b = lax.axis_index("blk")
    small = [
        pltpu.make_async_copy(x, y, tsem.at[i])
        for i, (x, y) in enumerate(
            (
                (owner_in, owner),
                (source_in, source),
                (target_in, target),
                (dsource_in, dsource),
                (dtarget_in, dtarget),
            )
        )
    ]
    large = [
        pltpu.make_async_copy(x, y, vsem.at[i])
        for i, (x, y) in enumerate(((loads_in, loads), (left_in, left), (right_in, right)))
    ]
    for copy in small + large:
        copy.start()
    zero[...] = jnp.zeros_like(zero)
    for d in range(PLANES):
        count[d] = 0
    for t in range(TARGETS):
        tables[HAS + t] = 0
        tables[LAST + t] = 0

    def clear(i, carry):
        seen[i] = 0
        return carry

    lax.fori_loop(0, len(FAR) * TARGETS, clear, 0, unroll=16)
    for copy in small:
        copy.wait()

    def tally(n, carry):
        t = dtarget[n]
        tables[HAS + t] = tables[HAS + t] + 1
        return carry

    lax.fori_loop(0, DENSE, tally, 0, unroll=4)
    start = jnp.int32(0)
    for t in range(TARGETS):
        tables[LAST + t] = start
        start = start + tables[HAS + t]

    def sort(n, carry):
        t = dtarget[n]
        spot = tables[LAST + t]
        tables[LAST + t] = spot + 1
        tables[ORDERED + spot] = n
        tables[SOURCED + spot] = dsource[n]
        tables[TARGETED + spot] = t
        return carry

    lax.fori_loop(0, DENSE, sort, 0, unroll=4)
    tables[SAME] = 0

    def link(s, carry):
        tables[SAME + s] = (tables[TARGETED + s] == tables[TARGETED + s - 1]).astype(jnp.int32)
        return carry

    lax.fori_loop(1, DENSE, link, 0, unroll=4)
    for t in range(TARGETS):
        tables[HAS + t] = jnp.minimum(tables[HAS + t], 1)

    length = jnp.int32(0)
    for i, d in enumerate(NEAR + (0,)):
        sender = lax.rem(b - d + PLANES, PLANES)

        def scan(n, carry, i=i, sender=sender):
            length, rank = carry
            tables[IDS + length] = target[sender, n]
            tables[SPOTS + length] = i * CAP + rank
            step = (owner[sender, n] == b).astype(jnp.int32)
            return length + step, rank + step

        length, _ = lax.fori_loop(0, LOW, scan, (length, jnp.int32(0)), unroll=8)
    for j in range(GROUP):
        tables[IDS + length + j] = 0
        tables[SPOTS + length + j] = NULL
    tables[LENGTH] = length

    for copy in large:
        copy.wait()

    def one(n, carry):
        d = lax.rem(owner[b, n] - b + PLANES, PLANES)
        r = count[d]
        count[d] = r + 1
        where[d * CAP + r] = target[b, n]
        coefficients = jnp.dot(left[n], loads[source[b, n]], preferred_element_type=F32)
        slots[d, r, :RANK, :] = right[n]
        slots[d, r, RANK:, :] = coefficients.astype(BF16)
        return carry

    lax.fori_loop(0, LOW, one, 0, unroll=8)
    whole = pltpu.make_async_copy(slots, slots_out, vsem.at[0])
    for d in FAR:
        amount = count[d]

        def blank(r, carry, d=d):
            slots[d, r] = jnp.zeros((2 * RANK, LEAF), BF16)
            where[d * CAP + r] = 0
            return carry

        lax.fori_loop(amount, lax.div(amount + GROUP - 1, GROUP) * GROUP, blank, 0)
    whole.start()

    for e, d in enumerate(FAR):

        @pl.loop(0, lax.div(count[d] + GROUP - 1, GROUP))
        def _(g):
            terms = [contribution(slots[d, g * GROUP + i]) for i in range(GROUP)]
            for i in range(GROUP):
                t = where[d * CAP + g * GROUP + i]
                first = seen[e * TARGETS + t] == 0
                seen[e * TARGETS + t] = 1
                acc[t] = jnp.where(first, terms[i], acc[t] + terms[i])

        @pl.loop(0, TARGETS)
        def _(t):
            has = seen[e * TARGETS + t] == 1

            @pl.when(has)
            def _():
                stage[e, t] = acc[t].astype(BF16)
                pltpu.make_async_copy(stage.at[e, t], far.at[e, t], sem.at[e]).start()

            @pl.when(jnp.logical_not(has))
            def _():
                pltpu.make_async_copy(zero, far.at[e, t], sem.at[e]).start()

    for e in range(len(FAR)):
        pltpu.make_async_copy(stage.at[e], far.at[e], sem.at[e]).wait()
    whole.wait()


def pack(owner, source, target, dsource, dtarget, loads, left, right):
    return pl.pallas_call(
        pack_kernel,
        out_shape=(
            jax.ShapeDtypeStruct((PLANES, CAP, 2 * RANK, LEAF), BF16),
            jax.ShapeDtypeStruct((len(FAR), TARGETS, CASES, LEAF), BF16),
            jax.ShapeDtypeStruct((TABLE,), jnp.int32),
        ),
        in_specs=[spec(pl.ANY)] * 8,
        out_specs=(spec(pl.ANY), spec(pl.ANY), spec(pltpu.SMEM)),
        scratch_shapes=[
            pltpu.SMEM((PLANES, LOW), jnp.int32),
            pltpu.SMEM((PLANES, LOW), jnp.int32),
            pltpu.SMEM((PLANES, LOW), jnp.int32),
            pltpu.SMEM((DENSE,), jnp.int32),
            pltpu.SMEM((DENSE,), jnp.int32),
            pltpu.VMEM((SOURCES, LEAF, CASES), BF16),
            pltpu.VMEM((LOW, RANK, LEAF), BF16),
            pltpu.VMEM((LOW, RANK, LEAF), BF16),
            pltpu.VMEM((PLANES, CAP, 2 * RANK, LEAF), BF16),
            pltpu.VMEM((TARGETS, CASES, LEAF), F32),
            pltpu.VMEM((len(FAR), TARGETS, CASES, LEAF), BF16),
            pltpu.VMEM((CASES, LEAF), BF16),
            pltpu.SMEM((PLANES,), jnp.int32),
            pltpu.SMEM((PLANES * CAP,), jnp.int32),
            pltpu.SMEM((len(FAR) * TARGETS,), jnp.int32),
            pltpu.SemaphoreType.DMA((5,)),
            pltpu.SemaphoreType.DMA((3,)),
            pltpu.SemaphoreType.DMA((len(FAR),)),
        ],
        compiler_params=pltpu.CompilerParams(vmem_limit_bytes=60 * MIB),
        name="pack",
    )(owner, source, target, dsource, dtarget, loads, left, right)


def reduce_scratch(dtype, local):
    return ([pltpu.VMEM((2, 4, 4, HALF, LEAF), dtype)] if local else []) + [
        pltpu.VMEM((2, 4, 4, HALF, LEAF), dtype),
        pltpu.VMEM((2, 4, HALF, LEAF), BF16),
        pltpu.VMEM((2, 2, 2, HALF, LEAF), BF16),
        pltpu.VMEM((2, 2, 4, HALF, LEAF), BF16),
        pltpu.VMEM((2, 2, 4, HALF, LEAF), BF16),
        pltpu.VMEM((2, 3, HALF, LEAF), BF16),
        pltpu.VMEM((2, 3, HALF, LEAF), BF16),
        pltpu.VMEM((2, HALF, LEAF), F32),
        pltpu.SemaphoreType.DMA((2, 4, 3)),
        pltpu.SemaphoreType.DMA((2, 2, 3, 2)),
        pltpu.SemaphoreType.DMA((2, 3, 2)),
    ]


ORDER = (2, 1, 3, 0)
SIDES = (1, 3)


class PlaneSum:
    def __init__(self, source, scratch, local):
        self.source = source
        self.own = scratch[0] if local else None
        (
            self.pair, self.across, self.passing, self.s1, self.r1, self.s2, self.r2, self.kept,
            self.csem, self.msem, self.nsem,
        ) = scratch[1:] if local else scratch
        self.b, self.y, self.x, self.k = place()

    def device(self, ax, d):
        y, x = self.y, self.x
        if ax == 0:
            x = lax.rem(x + d, 4)
        else:
            y = lax.rem(y + d, 4)
        return (self.b, (y * 4 + x) * 2 + self.k)

    def chunk(self, ax, d, core):
        rows = pl.ds(ax * HALF if self.own is not None else 0, HALF)
        if ax == 0:
            return self.source[ax].at[:, lax.rem(self.x + d, 4), core, rows, :]
        return self.source[ax].at[lax.rem(self.y + d, 4), :, core, rows, :]

    def local_copy(self, ax, d):
        return pltpu.make_async_copy(self.chunk(ax, d, self.k), self.own.at[ax, d], self.csem.at[ax, d, 0])

    def pair_copy(self, ax, d):
        return pltpu.make_async_remote_copy(
            src_ref=self.chunk(ax, d, 1 - self.k),
            dst_ref=self.pair.at[ax, d],
            send_sem=self.csem.at[ax, d, 1],
            recv_sem=self.csem.at[ax, d, 2],
            device_id=(self.b, (self.y * 4 + self.x) * 2 + 1 - self.k),
            device_id_type=MESH,
        )

    def begin(self):
        for d in ORDER:
            for ax in range(2):
                self.pair_copy(ax, d).start()
                if self.own is not None:
                    self.local_copy(ax, d).start()

    def arrived(self, ax, d):
        if self.own is not None:
            self.local_copy(ax, d).wait()
        self.pair_copy(ax, d).wait()

    def mine(self, ax, d, q):
        if self.own is not None:
            value = self.own[ax, d, q]
        elif ax == 0:
            value = self.source[ax][q, lax.rem(self.x + d, 4), self.k]
        else:
            value = self.source[ax][lax.rem(self.y + d, 4), q, self.k]
        return value.astype(F32) + self.pair[ax, d, q].astype(F32)

    def ring_copy(self, ax, side, part):
        low = 2 * side if part == 0 else 2 * side if part == 2 else 2 - 2 * side
        rows = pl.ds(low, 2)
        return pltpu.make_async_remote_copy(
            src_ref=self.across.at[ax, rows] if part == 0 else self.s1.at[ax, side, rows],
            dst_ref=self.passing.at[ax, side] if part == 0 else self.r1.at[ax, side, rows],
            send_sem=self.msem.at[ax, side, part, 0],
            recv_sem=self.msem.at[ax, side, part, 1],
            device_id=self.device(ax, SIDES[side]),
            device_id_type=MESH,
        )

    def last_copy(self, ax, d):
        return pltpu.make_async_remote_copy(
            src_ref=self.s2.at[ax, d - 1],
            dst_ref=self.r2.at[ax, d - 1],
            send_sem=self.nsem.at[ax, d - 1, 0],
            recv_sem=self.nsem.at[ax, d - 1, 1],
            device_id=self.device(1 - ax, d),
            device_id_type=MESH,
        )

    def opposite(self):
        for ax in range(2):
            self.arrived(ax, 2)
            for side in range(2):

                @pl.loop(2 * side, 2 * side + 2)
                def _(q):
                    self.across[ax, q] = self.mine(ax, 2, q).astype(BF16)

                self.ring_copy(ax, side, 0).start()

    def beside(self):
        for side in range(2):
            for ax in range(2):
                self.arrived(ax, SIDES[side])

                @pl.loop(2 - 2 * side, 4 - 2 * side)
                def _(q):
                    self.s1[ax, side, q] = self.mine(ax, SIDES[side], q).astype(BF16)

                self.ring_copy(ax, side, 1).start()

    def relay(self):
        for ax in range(2):
            for side in range(2):
                self.ring_copy(ax, side, 0).wait_recv()

                @pl.loop(0, 2)
                def _(p):
                    q = 2 * side + p
                    total = self.mine(ax, SIDES[side], q) + self.passing[ax, side, p].astype(F32)
                    self.s1[ax, side, q] = total.astype(BF16)

                self.ring_copy(ax, side, 2).start()

    def turn(self):
        for ax in range(2):
            self.arrived(ax, 0)
        for ax in range(2):
            for part in (1, 2):
                for side in range(2):
                    self.ring_copy(ax, side, part).wait_recv()
            here = self.y if ax == 0 else self.x
            for d in ORDER:
                q = lax.rem(here + d, 4)
                total = self.mine(ax, 0, q)
                for side in range(2):
                    total = total + self.r1[ax, side, q].astype(F32)
                if d == 0:
                    self.kept[ax] = total
                else:
                    self.s2[ax, d - 1] = total.astype(BF16)
                    self.last_copy(ax, d).start()

    def total(self, ax):
        for d in (1, 3, 2):
            self.last_copy(ax, d).wait_recv()
        total = self.kept[ax]
        for p in range(3):
            total = total + self.r2[ax, p].astype(F32)
        return total

    def finish(self):
        for ax in range(2):
            for side in range(2):
                for part in range(3):
                    self.ring_copy(ax, side, part).wait_send()
            for d in range(1, 4):
                self.last_copy(ax, d).wait_send()

    def partners(self):
        near = [self.device(ax, d) for ax in range(2) for d in range(1, 4)]
        return near + [(self.b, (self.y * 4 + self.x) * 2 + 1 - self.k)]


def greet(partners):
    barrier = pltpu.get_barrier_semaphore()
    for partner in partners:
        pl.semaphore_signal(barrier, inc=1, device_id=partner, device_id_type=MESH)
    pl.semaphore_wait(barrier, len(partners))


def exchange_kernel(slots, far, tables_in, loads_in, dense, received, results, sums0, sums1, *scratch):
    sums = (sums0, sums1)
    planes = [PlaneSum((far.at[e], far.at[e]), scratch[12 * e : 12 * e + 12], True) for e in range(len(FAR))]
    tables, loads, turned, blocks, running, zsem, lsem, dsem = scratch[36:]
    b = lax.axis_index("blk")
    c = lax.axis_index("col")

    def above(d):
        return (lax.rem(b + d, PLANES), c)

    own_slots = pltpu.make_async_copy(slots.at[0], received.at[pl.ds(len(NEAR) * CAP, CAP)], lsem.at[0])
    table_copy = pltpu.make_async_copy(tables_in, tables, lsem.at[1])
    load_copy = pltpu.make_async_copy(loads_in, loads, lsem.at[2])
    part = DENSE // PIECES
    dense_copies = [
        pltpu.make_async_copy(dense.at[pl.ds(p * part, part)], blocks.at[pl.ds(p * part, part)], dsem.at[p])
        for p in range(PIECES)
    ]
    greet(planes[0].partners() + [above(d) for d in NEAR])
    moves = [
        pltpu.make_async_remote_copy(
            src_ref=slots.at[d],
            dst_ref=received.at[pl.ds(i * CAP, CAP)],
            send_sem=zsem.at[i, 0],
            recv_sem=zsem.at[i, 1],
            device_id=above(d),
            device_id_type=MESH,
        )
        for i, d in enumerate(NEAR)
    ]
    for plane in planes[:1]:
        plane.begin()
    for move in moves:
        move.start()
    for plane in planes[1:]:
        plane.begin()
    for copy in [table_copy, load_copy, own_slots] + dense_copies:
        copy.start()
    received[NULL] = jnp.zeros((2 * RANK, LEAF), BF16)

    def dense_sums(half):
        running[0] = jnp.zeros((HALF, LEAF), F32)

        @pl.loop(0, DENSE // GROUP)
        def _(g):
            terms = [
                jnp.dot(
                    turned[tables[SOURCED + g * GROUP + i], half * HALF : (half + 1) * HALF, :],
                    blocks[tables[ORDERED + g * GROUP + i]],
                    preferred_element_type=F32,
                )
                for i in range(GROUP)
            ]
            total = running[g * GROUP]
            for i in range(GROUP):
                total = total * tables[SAME + g * GROUP + i].astype(F32) + terms[i]
                running[g * GROUP + i + 1] = total

        @pl.loop(0, TARGETS)
        def _(t):
            sums[half][t] = running[tables[LAST + t]] * tables[HAS + t].astype(F32)


    planes[0].opposite()
    planes[0].beside()
    planes[1].opposite()
    planes[1].beside()
    planes[0].relay()
    planes[2].opposite()
    planes[2].beside()
    load_copy.wait()
    table_copy.wait()
    for s in range(SOURCES):
        turned[s] = loads[s].T
    planes[1].relay()
    for copy in dense_copies:
        copy.wait()
    dense_sums(0)
    planes[0].turn()
    planes[2].relay()
    dense_sums(1)
    planes[1].turn()
    planes[2].turn()
    for e, plane in enumerate(planes):
        for ax in range(2):
            results[e, ax * HALF : (ax + 1) * HALF, :] = plane.total(ax).astype(BF16)
    for plane in planes:
        plane.finish()
    own_slots.wait()
    for move in moves:
        move.wait()


def exchange(slots, far, tables, loads, dense):
    scratch = []
    for _ in FAR:
        scratch += reduce_scratch(BF16, True)
    return pl.pallas_call(
        exchange_kernel,
        out_shape=(
            jax.ShapeDtypeStruct((NULL + 1, 2 * RANK, LEAF), BF16),
            jax.ShapeDtypeStruct((len(FAR), CASES, LEAF), BF16),
            jax.ShapeDtypeStruct((TARGETS, HALF, LEAF), F32),
            jax.ShapeDtypeStruct((TARGETS, HALF, LEAF), F32),
        ),
        in_specs=[spec(pl.ANY)] * 5,
        out_specs=(spec(pltpu.VMEM),) * 4,
        scratch_shapes=scratch
        + [
            pltpu.SMEM((TABLE,), jnp.int32),
            pltpu.VMEM((SOURCES, LEAF, CASES), BF16),
            pltpu.VMEM((SOURCES, CASES, LEAF), BF16),
            pltpu.VMEM((DENSE, LEAF, LEAF), BF16),
            pltpu.VMEM((DENSE + 1, HALF, LEAF), F32),
            pltpu.SemaphoreType.DMA((len(NEAR), 2)),
            pltpu.SemaphoreType.DMA((5,)),
            pltpu.SemaphoreType.DMA((PIECES,)),
        ],
        compiler_params=pltpu.CompilerParams(
            collective_id=1, has_side_effects=True, vmem_limit_bytes=42 * MIB
        ),
        name="exchange",
    )(slots, far, tables, loads, dense)


def gather_kernel(tables, received, in0, in1, sums0, sums1):
    @pl.loop(0, lax.div(tables[LENGTH] + GROUP - 1, GROUP))
    def _(g):
        terms = [contribution(received[tables[SPOTS + g * GROUP + i]]) for i in range(GROUP)]
        for i in range(GROUP):
            t = tables[IDS + g * GROUP + i]
            sums0[t] += terms[i][:HALF]
            sums1[t] += terms[i][HALF:]


def gather(tables, received, sums):
    return pl.pallas_call(
        gather_kernel,
        out_shape=(jax.ShapeDtypeStruct((TARGETS, HALF, LEAF), F32),) * 2,
        in_specs=[spec(pltpu.SMEM)] + [spec(pltpu.VMEM)] * 3,
        out_specs=(spec(pltpu.VMEM),) * 2,
        input_output_aliases={2: 0, 3: 1},
        compiler_params=pltpu.CompilerParams(vmem_limit_bytes=8 * MIB),
        name="gather",
    )(tables, received, *sums)


def final_kernel(source0, source1, results, out, *scratch):
    own = PlaneSum((source0, source1), scratch[:11], False)
    landed, zsem = scratch[11:]
    b = lax.axis_index("blk")
    c = lax.axis_index("col")

    def above(d):
        return (lax.rem(b + d, PLANES), c)

    greet(own.partners() + [above(d) for d in FAR])
    moves = [
        pltpu.make_async_remote_copy(
            src_ref=results.at[e],
            dst_ref=landed.at[e],
            send_sem=zsem.at[e, 0],
            recv_sem=zsem.at[e, 1],
            device_id=above(d),
            device_id_type=MESH,
        )
        for e, d in enumerate(FAR)
    ]
    own.begin()
    for move in moves:
        move.start()
    own.opposite()
    own.beside()
    own.relay()
    own.turn()
    for move in moves:
        move.wait()
    for ax in range(2):
        total = own.total(ax)
        for e in range(len(FAR)):
            total = total + landed[e, ax * HALF : (ax + 1) * HALF, :].astype(F32)
        out[:, ax * HALF : (ax + 1) * HALF] = total.T.astype(BF16)
    own.finish()


def final(sums, results):
    return pl.pallas_call(
        final_kernel,
        out_shape=jax.ShapeDtypeStruct((LEAF, CASES), BF16),
        in_specs=[spec(pltpu.VMEM)] * 3,
        out_specs=spec(pltpu.VMEM),
        scratch_shapes=reduce_scratch(F32, False)
        + [pltpu.VMEM((len(FAR), CASES, LEAF), BF16), pltpu.SemaphoreType.DMA((len(FAR), 2))],
        compiler_params=pltpu.CompilerParams(
            collective_id=2, has_side_effects=True, vmem_limit_bytes=16 * MIB
        ),
        name="final",
    )(*[x.reshape(4, 4, 2, HALF, LEAF) for x in sums], results)


def shards(
    loads,
    dense_blocks,
    dense_source,
    dense_target,
    left_factors,
    right_factors,
    block_owner,
    block_source,
    block_target,
):
    loads = loads.reshape(SOURCES, LEAF, CASES)
    owner = block_owner.reshape(PLANES, LOW)
    source = block_source.reshape(PLANES, LOW)
    target = block_target.reshape(PLANES, LOW)
    left = left_factors.reshape(LOW, RANK, LEAF)
    right = right_factors.reshape(LOW, RANK, LEAF)
    slots, far, tables = pack(
        owner, source, target, dense_source.reshape(DENSE), dense_target.reshape(DENSE), loads, left, right
    )
    received, results, *sums = exchange(
        slots, far.reshape(len(FAR), 4, 4, 2, CASES, LEAF), tables, loads, dense_blocks.reshape(DENSE, LEAF, LEAF)
    )
    sums = gather(tables, received, sums)
    return final(sums, results)


def solution(mesh):
    placed = (
        P("col", None),
        P("blk", "col", None, None, None),
        P("blk", "col", None),
        P("blk", "col", None),
        P("blk", "col", None, None, None),
        P("blk", "col", None, None, None),
        P(None, "col", None, None),
        P(None, "col", None),
        P(None, "col", None),
    )
    return jax.shard_map(
        shards, mesh=mesh, in_specs=placed, out_specs=P(("blk", "col"), None), check_vma=False
    )
```

```python
import jax
import jax.numpy as jnp
from jax import lax
from jax.experimental import pallas as pl
from jax.experimental.pallas import tpu as pltpu
from jax.sharding import PartitionSpec as P

LEAF = 256
HALF = 128
QUARTER = 64
CASES = 256
RANK = 32
SOURCES = 8
TARGETS = 32
DENSE = 60
LOW = 64
CAP = 16
PLANES = 8
GROUP = 4
PIECES = 4
ORDERED = 0
SOURCED = 64
TARGETED = 128
LAST = 256
HAS = 288
IDS = 320
SPOTS = 416
LENGTH = 508
FAR_ORDER = 512
FAR_TARGET = 560
FAR_LAST = 608
TABLE = 768
NULL = 80
NEAR = (1, 7, 2, 6)
FAR = (4, 3, 5)
MESH = pl.DeviceIdType.MESH
MIB = 1 << 20
BF16 = jnp.bfloat16
F32 = jnp.float32


def spec(space):
    return pl.BlockSpec(memory_space=space)


def place():
    b = lax.axis_index("blk")
    c = lax.axis_index("col")
    return b, lax.div(c, 8), lax.rem(lax.div(c, 2), 4), lax.rem(c, 2)


def contribution(pair):
    return lax.dot_general(
        pair[RANK:], pair[:RANK], (((0,), (0,)), ((), ())), preferred_element_type=F32
    )


def pack_kernel(
    owner_in, source_in, target_in, dsource_in, dtarget_in, loads_in, left_in, right_in, slots_out, tables,
    owner, source, target, dsource, dtarget, loads, left, right, slots, count, where, tsem, vsem,
):
    b = lax.axis_index("blk")
    small = [
        pltpu.make_async_copy(x, y, tsem.at[i])
        for i, (x, y) in enumerate(
            (
                (owner_in, owner),
                (source_in, source),
                (target_in, target),
                (dsource_in, dsource),
                (dtarget_in, dtarget),
            )
        )
    ]
    large = [
        pltpu.make_async_copy(x, y, vsem.at[i])
        for i, (x, y) in enumerate(((loads_in, loads), (left_in, left), (right_in, right)))
    ]
    for copy in small + large:
        copy.start()
    for d in range(PLANES):
        count[d] = 0
    for t in range(TARGETS):
        tables[HAS + t] = 0
        tables[LAST + t] = 0

    def clear(i, carry):
        tables[FAR_LAST + i] = 0
        return carry

    lax.fori_loop(0, len(FAR) * TARGETS, clear, 0, unroll=16)

    def blank(i, carry):
        tables[FAR_ORDER + i] = 0
        tables[FAR_TARGET + i] = 0
        return carry

    lax.fori_loop(0, len(FAR) * CAP, blank, 0, unroll=16)
    for copy in small:
        copy.wait()

    def tally(n, carry):
        t = dtarget[n]
        tables[HAS + t] = tables[HAS + t] + 1
        return carry

    lax.fori_loop(0, DENSE, tally, 0, unroll=4)
    start = jnp.int32(0)
    for t in range(TARGETS):
        tables[LAST + t] = start
        start = start + tables[HAS + t]

    def sort(n, carry):
        t = dtarget[n]
        spot = tables[LAST + t]
        tables[LAST + t] = spot + 1
        tables[ORDERED + spot] = n
        tables[SOURCED + spot] = dsource[n]
        tables[TARGETED + spot] = t
        return carry

    lax.fori_loop(0, DENSE, sort, 0, unroll=4)
    for t in range(TARGETS):
        tables[HAS + t] = jnp.minimum(tables[HAS + t], 1)

    length = jnp.int32(0)
    for i, d in enumerate(NEAR + (0,)):
        sender = lax.rem(b - d + PLANES, PLANES)

        def scan(n, carry, i=i, sender=sender):
            length, rank = carry
            tables[IDS + length] = target[sender, n]
            tables[SPOTS + length] = i * CAP + rank
            step = (owner[sender, n] == b).astype(jnp.int32)
            return length + step, rank + step

        length, _ = lax.fori_loop(0, LOW, scan, (length, jnp.int32(0)), unroll=8)
    for j in range(GROUP):
        tables[IDS + length + j] = 0
        tables[SPOTS + length + j] = NULL
    tables[LENGTH] = length

    for copy in large:
        copy.wait()

    def one(n, carry):
        d = lax.rem(owner[b, n] - b + PLANES, PLANES)
        r = count[d]
        count[d] = r + 1
        where[d * CAP + r] = target[b, n]
        coefficients = jnp.dot(left[n], loads[source[b, n]], preferred_element_type=F32)
        slots[d, r, :RANK, :] = right[n]
        slots[d, r, RANK:, :] = coefficients.astype(BF16)
        return carry

    lax.fori_loop(0, LOW, one, 0, unroll=8)
    whole = pltpu.make_async_copy(slots, slots_out, vsem.at[0])
    whole.start()

    for e, d in enumerate(FAR):
        amount = count[d]

        def add(r, carry, e=e, d=d):
            t = where[d * CAP + r]
            tables[FAR_LAST + e * TARGETS + t] = tables[FAR_LAST + e * TARGETS + t] + 1
            return carry

        lax.fori_loop(0, amount, add, 0)

        def begin(t, start, e=e):
            held = tables[FAR_LAST + e * TARGETS + t]
            tables[FAR_LAST + e * TARGETS + t] = start
            return start + held

        lax.fori_loop(0, TARGETS, begin, jnp.int32(0), unroll=8)

        def put(r, carry, e=e, d=d):
            t = where[d * CAP + r]
            spot = tables[FAR_LAST + e * TARGETS + t]
            tables[FAR_LAST + e * TARGETS + t] = spot + 1
            tables[FAR_ORDER + e * CAP + spot] = r
            tables[FAR_TARGET + e * CAP + spot] = t
            return carry

        lax.fori_loop(0, amount, put, 0)

        def last(t, before, e=e):
            end = tables[FAR_LAST + e * TARGETS + t]
            tables[FAR_LAST + e * TARGETS + t] = jnp.where(end == before, 0, end)
            return end

        lax.fori_loop(0, TARGETS, last, jnp.int32(0), unroll=8)

    whole.wait()


def pack(owner, source, target, dsource, dtarget, loads, left, right):
    return pl.pallas_call(
        pack_kernel,
        out_shape=(
            jax.ShapeDtypeStruct((PLANES, CAP, 2 * RANK, LEAF), BF16),
            jax.ShapeDtypeStruct((TABLE,), jnp.int32),
        ),
        in_specs=[spec(pl.ANY)] * 8,
        out_specs=(spec(pl.ANY), spec(pltpu.SMEM)),
        scratch_shapes=[
            pltpu.SMEM((PLANES, LOW), jnp.int32),
            pltpu.SMEM((PLANES, LOW), jnp.int32),
            pltpu.SMEM((PLANES, LOW), jnp.int32),
            pltpu.SMEM((DENSE,), jnp.int32),
            pltpu.SMEM((DENSE,), jnp.int32),
            pltpu.VMEM((SOURCES, LEAF, CASES), BF16),
            pltpu.VMEM((LOW, RANK, LEAF), BF16),
            pltpu.VMEM((LOW, RANK, LEAF), BF16),
            pltpu.VMEM((PLANES, CAP, 2 * RANK, LEAF), BF16),
            pltpu.SMEM((PLANES,), jnp.int32),
            pltpu.SMEM((PLANES * CAP,), jnp.int32),
            pltpu.SemaphoreType.DMA((5,)),
            pltpu.SemaphoreType.DMA((3,)),
        ],
        compiler_params=pltpu.CompilerParams(vmem_limit_bytes=60 * MIB),
        name="pack",
    )(owner, source, target, dsource, dtarget, loads, left, right)


def reduce_scratch(dtype, local):
    return [pltpu.VMEM((2, 4 if local else 3, 4, HALF, LEAF), BF16)] + [
        pltpu.VMEM((2, 4, 4, HALF, LEAF), dtype),
        pltpu.VMEM((2, 2, 2, HALF, LEAF), BF16),
        pltpu.VMEM((2, 2, 4, HALF, LEAF), BF16),
        pltpu.VMEM((2, 3, HALF, LEAF), BF16),
        pltpu.VMEM((2, 3, HALF, LEAF), BF16),
        pltpu.VMEM((2, HALF, LEAF), F32),
        pltpu.SemaphoreType.DMA((2, 4, 3)),
        pltpu.SemaphoreType.DMA((2, 2, 3, 2)),
        pltpu.SemaphoreType.DMA((2, 3, 2)),
    ]


ORDER = (2, 1, 3, 0)
SIDES = (1, 3)


class PlaneSum:
    def __init__(self, source, scratch, give):
        local = give is not None
        self.source = source
        self.give = give
        self.given = False
        self.own = scratch[0] if local else None
        self.sent = scratch[0]
        (
            self.pair, self.passing, self.r1, self.s2, self.r2, self.kept,
            self.csem, self.msem, self.nsem,
        ) = scratch[1:]
        self.b, self.y, self.x, self.k = place()

    def device(self, ax, d):
        y, x = self.y, self.x
        if ax == 0:
            x = lax.rem(x + d, 4)
        else:
            y = lax.rem(y + d, 4)
        return (self.b, (y * 4 + x) * 2 + self.k)

    def chunk(self, ax, d, core):
        if self.give is not None:
            return self.give.at[ax, d]
        if ax == 0:
            return self.source[ax].at[:, lax.rem(self.x + d, 4), core]
        return self.source[ax].at[lax.rem(self.y + d, 4), :, core]

    def pair_copy(self, ax, d):
        return pltpu.make_async_remote_copy(
            src_ref=self.chunk(ax, d, 1 - self.k),
            dst_ref=self.pair.at[ax, d],
            send_sem=self.csem.at[ax, d, 1],
            recv_sem=self.csem.at[ax, d, 2],
            device_id=(self.b, (self.y * 4 + self.x) * 2 + 1 - self.k),
            device_id_type=MESH,
        )

    def begin(self):
        for d in ORDER:
            for ax in range(2):
                self.pair_copy(ax, d).start()

    def form(self, tables, e, slots, running):
        for h in range(4):
            running[h] = jnp.zeros((QUARTER, LEAF), F32)

        @pl.loop(0, CAP // GROUP)
        def _(g):
            terms = [contribution(slots[tables[FAR_ORDER + e * CAP + g * GROUP + i]]) for i in range(GROUP)]
            for h in range(4):
                total = running[4 * GROUP * g + h]
                for i in range(GROUP):
                    s = g * GROUP + i
                    here = tables[FAR_TARGET + e * CAP + s]
                    same = (here == tables[FAR_TARGET + e * CAP + s - 1]).astype(jnp.int32)
                    total = total * same.astype(F32) + terms[i][h * QUARTER : (h + 1) * QUARTER]
                    running[4 * (s + 1) + h] = total

        for d in ORDER:
            for ax in range(2):

                @pl.loop(0, 4)
                def _(q):
                    place = (q * 4 + lax.rem(self.x + d, 4)) if ax == 0 else (lax.rem(self.y + d, 4) * 4 + q)
                    first = FAR_LAST + e * TARGETS + place * 2
                    for ref, core in ((self.give, 1 - self.k), (self.own, self.k)):
                        spot = 4 * tables[first + core] + 2 * ax
                        for h in range(2):
                            ref[ax, d, q, h * QUARTER : (h + 1) * QUARTER, :] = running[spot + h].astype(BF16)

                self.pair_copy(ax, d).start()

    def arrived(self, ax, d):
        self.pair_copy(ax, d).wait_recv()

    def gave(self):
        if not self.given:
            for d in ORDER:
                for ax in range(2):
                    self.pair_copy(ax, d).wait_send()
        self.given = True

    def out(self, ax, d):
        return self.sent.at[ax, d if self.own is not None else d - 1]

    def mine(self, ax, d, q):
        if self.own is not None:
            value = self.own[ax, d, q]
        elif ax == 0:
            value = self.source[ax][q, lax.rem(self.x + d, 4), self.k]
        else:
            value = self.source[ax][lax.rem(self.y + d, 4), q, self.k]
        return value.astype(F32) + self.pair[ax, d, q].astype(F32)

    def ring_copy(self, ax, side, part):
        low = 2 * side if part == 0 else 2 * side if part == 2 else 2 - 2 * side
        rows = pl.ds(low, 2)
        return pltpu.make_async_remote_copy(
            src_ref=self.out(ax, 2 if part == 0 else SIDES[side]).at[rows],
            dst_ref=self.passing.at[ax, side] if part == 0 else self.r1.at[ax, side, rows],
            send_sem=self.msem.at[ax, side, part, 0],
            recv_sem=self.msem.at[ax, side, part, 1],
            device_id=self.device(ax, SIDES[side]),
            device_id_type=MESH,
        )

    def last_copy(self, ax, d):
        return pltpu.make_async_remote_copy(
            src_ref=self.s2.at[ax, d - 1],
            dst_ref=self.r2.at[ax, d - 1],
            send_sem=self.nsem.at[ax, d - 1, 0],
            recv_sem=self.nsem.at[ax, d - 1, 1],
            device_id=self.device(1 - ax, d),
            device_id_type=MESH,
        )

    def opposite(self):
        for ax in range(2):
            self.arrived(ax, 2)
            for side in range(2):

                @pl.loop(2 * side, 2 * side + 2)
                def _(q):
                    self.out(ax, 2)[q] = self.mine(ax, 2, q).astype(BF16)

                self.ring_copy(ax, side, 0).start()

    def beside(self):
        for side in range(2):
            for ax in range(2):
                self.arrived(ax, SIDES[side])

                @pl.loop(2 - 2 * side, 4 - 2 * side)
                def _(q):
                    self.out(ax, SIDES[side])[q] = self.mine(ax, SIDES[side], q).astype(BF16)

                self.ring_copy(ax, side, 1).start()

    def relay(self):
        for ax in range(2):
            for side in range(2):
                self.ring_copy(ax, side, 0).wait_recv()

                @pl.loop(0, 2)
                def _(p):
                    q = 2 * side + p
                    total = self.mine(ax, SIDES[side], q) + self.passing[ax, side, p].astype(F32)
                    self.out(ax, SIDES[side])[q] = total.astype(BF16)

                self.ring_copy(ax, side, 2).start()

    def turn(self):
        for ax in range(2):
            self.arrived(ax, 0)
        for ax in range(2):
            for part in (1, 2):
                for side in range(2):
                    self.ring_copy(ax, side, part).wait_recv()
            here = self.y if ax == 0 else self.x
            for d in ORDER:
                q = lax.rem(here + d, 4)
                total = self.mine(ax, 0, q)
                for side in range(2):
                    total = total + self.r1[ax, side, q].astype(F32)
                if d == 0:
                    self.kept[ax] = total
                else:
                    self.s2[ax, d - 1] = total.astype(BF16)
                    self.last_copy(ax, d).start()

    def total(self, ax):
        for d in (1, 3, 2):
            self.last_copy(ax, d).wait_recv()
        total = self.kept[ax]
        for p in range(3):
            total = total + self.r2[ax, p].astype(F32)
        return total

    def finish(self):
        self.gave()
        for ax in range(2):
            for side in range(2):
                for part in range(3):
                    self.ring_copy(ax, side, part).wait_send()
            for d in range(1, 4):
                self.last_copy(ax, d).wait_send()

    def partners(self):
        near = [self.device(ax, d) for ax in range(2) for d in range(1, 4)]
        return near + [(self.b, (self.y * 4 + self.x) * 2 + 1 - self.k)]


def greet(partners):
    barrier = pltpu.get_barrier_semaphore()
    for partner in partners:
        pl.semaphore_signal(barrier, inc=1, device_id=partner, device_id_type=MESH)
    pl.semaphore_wait(barrier, len(partners))


def exchange_kernel(slots, tables_in, loads, dense, received, results, sums0, sums1, *scratch):
    sums = (sums0, sums1)
    gives = scratch[30:32]
    planes = [PlaneSum(None, scratch[10 * e : 10 * e + 10], gives[e % 2]) for e in range(len(FAR))]
    far_slots = scratch[32:35]
    tables, turned, blocks, running, zsem, lsem, dsem = scratch[35:]
    b = lax.axis_index("blk")
    c = lax.axis_index("col")

    def above(d):
        return (lax.rem(b + d, PLANES), c)

    own_slots = pltpu.make_async_copy(slots.at[0], received.at[pl.ds(len(NEAR) * CAP, CAP)], lsem.at[0])
    table_copy = pltpu.make_async_copy(tables_in, tables, lsem.at[1])
    far_copies = [
        pltpu.make_async_copy(slots.at[d], far_slots[e], lsem.at[2 + e]) for e, d in enumerate(FAR)
    ]
    part = DENSE // PIECES
    dense_copies = [
        pltpu.make_async_copy(dense.at[pl.ds(p * part, part)], blocks.at[pl.ds(p * part, part)], dsem.at[p])
        for p in range(PIECES)
    ]
    for copy in [table_copy] + far_copies:
        copy.start()
    greet(planes[0].partners() + [above(d) for d in NEAR])
    moves = [
        pltpu.make_async_remote_copy(
            src_ref=slots.at[d],
            dst_ref=received.at[pl.ds(i * CAP, CAP)],
            send_sem=zsem.at[i, 0],
            recv_sem=zsem.at[i, 1],
            device_id=above(d),
            device_id_type=MESH,
        )
        for i, d in enumerate(NEAR)
    ]
    for move in moves:
        move.start()
    for copy in [own_slots] + dense_copies:
        copy.start()
    received[NULL] = jnp.zeros((2 * RANK, LEAF), BF16)

    def dense_sums(part):
        low = part * QUARTER
        running[0] = jnp.zeros((QUARTER, LEAF), F32)

        @pl.loop(0, DENSE // GROUP)
        def _(g):
            terms = [
                jnp.dot(
                    turned[tables[SOURCED + g * GROUP + i], low : low + QUARTER, :],
                    blocks[tables[ORDERED + g * GROUP + i]],
                    preferred_element_type=F32,
                )
                for i in range(GROUP)
            ]
            total = running[g * GROUP]
            for i in range(GROUP):
                here = tables[TARGETED + g * GROUP + i]
                same = (here == tables[TARGETED + g * GROUP + i - 1]).astype(jnp.int32)
                total = total * same.astype(F32) + terms[i]
                running[g * GROUP + i + 1] = total

        @pl.loop(0, TARGETS)
        def _(t):
            sums[low // HALF][t, low % HALF : low % HALF + QUARTER, :] = running[tables[LAST + t]] * tables[HAS + t].astype(F32)


    table_copy.wait()
    for e, plane in enumerate(planes):
        far_copies[e].wait()
        if e == 2:
            planes[0].gave()
        plane.form(tables, e, far_slots[e], running)
        plane.opposite()
        plane.beside()
        if e == 1:
            planes[0].relay()
    for s in range(SOURCES):
        turned[s] = loads[s].T
    planes[1].relay()
    for copy in dense_copies:
        copy.wait()
    dense_sums(0)
    dense_sums(1)
    planes[0].turn()
    planes[2].relay()
    dense_sums(2)
    dense_sums(3)
    planes[1].turn()
    planes[2].turn()
    for e, plane in enumerate(planes):
        for ax in range(2):
            results[e, ax * HALF : (ax + 1) * HALF, :] = plane.total(ax).astype(BF16)
    for plane in planes:
        plane.finish()
    own_slots.wait()
    for move in moves:
        move.wait()


def exchange(slots, tables, loads, dense):
    scratch = []
    for _ in FAR:
        scratch += reduce_scratch(BF16, True)
    return pl.pallas_call(
        exchange_kernel,
        out_shape=(
            jax.ShapeDtypeStruct((NULL + 1, 2 * RANK, LEAF), BF16),
            jax.ShapeDtypeStruct((len(FAR), CASES, LEAF), BF16),
            jax.ShapeDtypeStruct((TARGETS, HALF, LEAF), F32),
            jax.ShapeDtypeStruct((TARGETS, HALF, LEAF), F32),
        ),
        in_specs=[spec(pl.ANY), spec(pl.ANY), spec(pltpu.VMEM), spec(pl.ANY)],
        out_specs=(spec(pltpu.VMEM),) * 4,
        scratch_shapes=scratch
        + [pltpu.VMEM((2, 4, 4, HALF, LEAF), BF16)] * 2
        + [pltpu.VMEM((CAP, 2 * RANK, LEAF), BF16)] * len(FAR)
        + [
            pltpu.SMEM((TABLE,), jnp.int32),
            pltpu.VMEM((SOURCES, CASES, LEAF), BF16),
            pltpu.VMEM((DENSE, LEAF, LEAF), BF16),
            pltpu.VMEM((4 * (CAP + 1), QUARTER, LEAF), F32),
            pltpu.SemaphoreType.DMA((len(NEAR), 2)),
            pltpu.SemaphoreType.DMA((5,)),
            pltpu.SemaphoreType.DMA((PIECES,)),
        ],
        compiler_params=pltpu.CompilerParams(
            collective_id=1, has_side_effects=True, vmem_limit_bytes=40 * MIB
        ),
        name="exchange",
    )(slots, tables, loads, dense)


def gather_kernel(tables, received, in0, in1, sums0, sums1):
    @pl.loop(0, lax.div(tables[LENGTH] + GROUP - 1, GROUP))
    def _(g):
        terms = [contribution(received[tables[SPOTS + g * GROUP + i]]) for i in range(GROUP)]
        for i in range(GROUP):
            t = tables[IDS + g * GROUP + i]
            sums0[t] += terms[i][:HALF]
            sums1[t] += terms[i][HALF:]


def gather(tables, received, sums):
    return pl.pallas_call(
        gather_kernel,
        out_shape=(jax.ShapeDtypeStruct((TARGETS, HALF, LEAF), F32),) * 2,
        in_specs=[spec(pltpu.SMEM)] + [spec(pltpu.VMEM)] * 3,
        out_specs=(spec(pltpu.VMEM),) * 2,
        input_output_aliases={2: 0, 3: 1},
        compiler_params=pltpu.CompilerParams(vmem_limit_bytes=8 * MIB),
        name="gather",
    )(tables, received, *sums)


def final_kernel(source0, source1, results, out, *scratch):
    own = PlaneSum((source0, source1), scratch[:10], None)
    landed, zsem = scratch[10:]
    b = lax.axis_index("blk")
    c = lax.axis_index("col")

    def above(d):
        return (lax.rem(b + d, PLANES), c)

    greet(own.partners() + [above(d) for d in FAR])
    moves = [
        pltpu.make_async_remote_copy(
            src_ref=results.at[e],
            dst_ref=landed.at[e],
            send_sem=zsem.at[e, 0],
            recv_sem=zsem.at[e, 1],
            device_id=above(d),
            device_id_type=MESH,
        )
        for e, d in enumerate(FAR)
    ]
    own.begin()
    for move in moves:
        move.start()
    own.opposite()
    own.beside()
    own.relay()
    own.turn()
    for move in moves:
        move.wait()
    for ax in range(2):
        total = own.total(ax)
        for e in range(len(FAR)):
            total = total + landed[e, ax * HALF : (ax + 1) * HALF, :].astype(F32)
        out[:, ax * HALF : (ax + 1) * HALF] = total.T.astype(BF16)
    own.finish()


def final(sums, results):
    return pl.pallas_call(
        final_kernel,
        out_shape=jax.ShapeDtypeStruct((LEAF, CASES), BF16),
        in_specs=[spec(pltpu.VMEM)] * 3,
        out_specs=spec(pltpu.VMEM),
        scratch_shapes=reduce_scratch(F32, False)
        + [pltpu.VMEM((len(FAR), CASES, LEAF), BF16), pltpu.SemaphoreType.DMA((len(FAR), 2))],
        compiler_params=pltpu.CompilerParams(
            collective_id=2, has_side_effects=True, vmem_limit_bytes=16 * MIB
        ),
        name="final",
    )(*[x.reshape(4, 4, 2, HALF, LEAF) for x in sums], results)


def shards(
    loads,
    dense_blocks,
    dense_source,
    dense_target,
    left_factors,
    right_factors,
    block_owner,
    block_source,
    block_target,
):
    loads = loads.reshape(SOURCES, LEAF, CASES)
    owner = block_owner.reshape(PLANES, LOW)
    source = block_source.reshape(PLANES, LOW)
    target = block_target.reshape(PLANES, LOW)
    left = left_factors.reshape(LOW, RANK, LEAF)
    right = right_factors.reshape(LOW, RANK, LEAF)
    slots, tables = pack(
        owner, source, target, dense_source.reshape(DENSE), dense_target.reshape(DENSE), loads, left, right
    )
    received, results, *sums = exchange(slots, tables, loads, dense_blocks.reshape(DENSE, LEAF, LEAF))
    sums = gather(tables, received, sums)
    return final(sums, results)


def solution(mesh):
    placed = (
        P("col", None),
        P("blk", "col", None, None, None),
        P("blk", "col", None),
        P("blk", "col", None),
        P("blk", "col", None, None, None),
        P("blk", "col", None, None, None),
        P(None, "col", None, None),
        P(None, "col", None),
        P(None, "col", None),
    )
    return jax.shard_map(
        shards, mesh=mesh, in_specs=placed, out_specs=P(("blk", "col"), None), check_vma=False
    )
```

```python
import jax
import jax.numpy as jnp
from jax import lax
from jax.experimental import pallas as pl
from jax.experimental.pallas import tpu as pltpu
from jax.sharding import PartitionSpec as P

LEAF = 256
HALF = 128
QUARTER = 64
CASES = 256
RANK = 32
SOURCES = 8
TARGETS = 32
DENSE = 60
LOW = 64
CAP = 16
PLANES = 8
GROUP = 4
NEAR_GROUP = 8
PIECES = 4
ORDERED = 0
SOURCED = 64
TARGETED = 128
LAST = 256
HAS = 288
IDS = 320
SPOTS = 416
LENGTH = 508
FAR_ORDER = 512
FAR_TARGET = 560
FAR_LAST = 608
TABLE = 768
NULL = 80
NEAR = (1, 7, 2, 6)
FAR = (4, 3, 5)
MESH = pl.DeviceIdType.MESH
MIB = 1 << 20
BF16 = jnp.bfloat16
F32 = jnp.float32


def spec(space):
    return pl.BlockSpec(memory_space=space)


def place():
    b = lax.axis_index("blk")
    c = lax.axis_index("col")
    return b, lax.div(c, 8), lax.rem(lax.div(c, 2), 4), lax.rem(c, 2)


def contribution(pair):
    return lax.dot_general(
        pair[RANK:], pair[:RANK], (((0,), (0,)), ((), ())), preferred_element_type=F32
    )


def pack_kernel(
    owner_in, source_in, target_in, dsource_in, dtarget_in, loads_in, left_in, right_in, slots_out, tables,
    owner, source, target, dsource, dtarget, loads, left, right, slots, count, where, tsem, vsem,
):
    b = lax.axis_index("blk")
    small = [
        pltpu.make_async_copy(x, y, tsem.at[i])
        for i, (x, y) in enumerate(
            (
                (owner_in, owner),
                (source_in, source),
                (target_in, target),
                (dsource_in, dsource),
                (dtarget_in, dtarget),
            )
        )
    ]
    large = [
        pltpu.make_async_copy(x, y, vsem.at[i])
        for i, (x, y) in enumerate(((loads_in, loads), (left_in, left), (right_in, right)))
    ]
    for copy in small + large:
        copy.start()
    for d in range(PLANES):
        count[d] = 0
    for t in range(TARGETS):
        tables[HAS + t] = 0
        tables[LAST + t] = 0

    def clear(i, carry):
        tables[FAR_LAST + i] = 0
        return carry

    lax.fori_loop(0, len(FAR) * TARGETS, clear, 0, unroll=16)

    def blank(i, carry):
        tables[FAR_ORDER + i] = 0
        tables[FAR_TARGET + i] = 0
        return carry

    lax.fori_loop(0, len(FAR) * CAP, blank, 0, unroll=16)
    for copy in small:
        copy.wait()

    def tally(n, carry):
        t = dtarget[n]
        tables[HAS + t] = tables[HAS + t] + 1
        return carry

    lax.fori_loop(0, DENSE, tally, 0, unroll=4)
    start = jnp.int32(0)
    for t in range(TARGETS):
        tables[LAST + t] = start
        start = start + tables[HAS + t]

    def sort(n, carry):
        t = dtarget[n]
        spot = tables[LAST + t]
        tables[LAST + t] = spot + 1
        tables[ORDERED + spot] = n
        tables[SOURCED + spot] = dsource[n]
        tables[TARGETED + spot] = t
        return carry

    lax.fori_loop(0, DENSE, sort, 0, unroll=4)
    for t in range(TARGETS):
        tables[HAS + t] = jnp.minimum(tables[HAS + t], 1)

    for copy in large:
        copy.wait()

    senders = [lax.rem(b - d + PLANES, PLANES) for d in NEAR + (0,)]

    def one(n, carry):
        d = lax.rem(owner[b, n] - b + PLANES, PLANES)
        r = count[d]
        count[d] = r + 1
        where[d * CAP + r] = target[b, n]
        coefficients = jnp.dot(left[n], loads[source[b, n]], preferred_element_type=F32)
        slots[d, r, :RANK, :] = right[n]
        slots[d, r, RANK:, :] = coefficients.astype(BF16)
        length, *ranks = carry
        for i, sender in enumerate(senders):
            tables[IDS + length] = target[sender, n]
            tables[SPOTS + length] = i * CAP + ranks[i]
            step = (owner[sender, n] == b).astype(jnp.int32)
            length = length + step
            ranks[i] = ranks[i] + step
        return (length, *ranks)

    length, *_ = lax.fori_loop(0, LOW, one, (jnp.int32(0),) * (2 + len(NEAR)), unroll=8)
    for j in range(NEAR_GROUP):
        tables[IDS + length + j] = 0
        tables[SPOTS + length + j] = NULL
    tables[LENGTH] = length
    whole = pltpu.make_async_copy(slots, slots_out, vsem.at[0])
    whole.start()

    for e, d in enumerate(FAR):
        amount = count[d]

        def add(r, carry, e=e, d=d):
            t = where[d * CAP + r]
            tables[FAR_LAST + e * TARGETS + t] = tables[FAR_LAST + e * TARGETS + t] + 1
            return carry

        lax.fori_loop(0, amount, add, 0)

        def begin(t, start, e=e):
            held = tables[FAR_LAST + e * TARGETS + t]
            tables[FAR_LAST + e * TARGETS + t] = start
            return start + held

        lax.fori_loop(0, TARGETS, begin, jnp.int32(0), unroll=8)

        def put(r, carry, e=e, d=d):
            t = where[d * CAP + r]
            spot = tables[FAR_LAST + e * TARGETS + t]
            tables[FAR_LAST + e * TARGETS + t] = spot + 1
            tables[FAR_ORDER + e * CAP + spot] = r
            tables[FAR_TARGET + e * CAP + spot] = t
            return carry

        lax.fori_loop(0, amount, put, 0)

        def last(t, before, e=e):
            end = tables[FAR_LAST + e * TARGETS + t]
            tables[FAR_LAST + e * TARGETS + t] = jnp.where(end == before, 0, end)
            return end

        lax.fori_loop(0, TARGETS, last, jnp.int32(0), unroll=8)

    whole.wait()


def pack(owner, source, target, dsource, dtarget, loads, left, right):
    return pl.pallas_call(
        pack_kernel,
        out_shape=(
            jax.ShapeDtypeStruct((PLANES, CAP, 2 * RANK, LEAF), BF16),
            jax.ShapeDtypeStruct((TABLE,), jnp.int32),
        ),
        in_specs=[spec(pl.ANY)] * 8,
        out_specs=(spec(pl.ANY), spec(pltpu.SMEM)),
        scratch_shapes=[
            pltpu.SMEM((PLANES, LOW), jnp.int32),
            pltpu.SMEM((PLANES, LOW), jnp.int32),
            pltpu.SMEM((PLANES, LOW), jnp.int32),
            pltpu.SMEM((DENSE,), jnp.int32),
            pltpu.SMEM((DENSE,), jnp.int32),
            pltpu.VMEM((SOURCES, LEAF, CASES), BF16),
            pltpu.VMEM((LOW, RANK, LEAF), BF16),
            pltpu.VMEM((LOW, RANK, LEAF), BF16),
            pltpu.VMEM((PLANES, CAP, 2 * RANK, LEAF), BF16),
            pltpu.SMEM((PLANES,), jnp.int32),
            pltpu.SMEM((PLANES * CAP,), jnp.int32),
            pltpu.SemaphoreType.DMA((5,)),
            pltpu.SemaphoreType.DMA((3,)),
        ],
        compiler_params=pltpu.CompilerParams(vmem_limit_bytes=60 * MIB),
        name="pack",
    )(owner, source, target, dsource, dtarget, loads, left, right)


def reduce_scratch(dtype, local):
    return [pltpu.VMEM((2, 4 if local else 3, 4, HALF, LEAF), BF16)] + [
        pltpu.VMEM((2, 4, 4, HALF, LEAF), dtype),
        pltpu.VMEM((2, 2, 2, HALF, LEAF), BF16),
        pltpu.VMEM((2, 2, 4, HALF, LEAF), BF16),
        pltpu.VMEM((2, 3, HALF, LEAF), BF16),
        pltpu.VMEM((2, 3, HALF, LEAF), BF16),
        pltpu.VMEM((2, HALF, LEAF), F32),
        pltpu.SemaphoreType.DMA((2, 4, 3)),
        pltpu.SemaphoreType.DMA((2, 2, 3, 2)),
        pltpu.SemaphoreType.DMA((2, 3, 2)),
    ]


ORDER = (2, 1, 3, 0)
SIDES = (1, 3)


class PlaneSum:
    def __init__(self, source, scratch, give):
        local = give is not None
        self.source = source
        self.give = give
        self.given = False
        self.own = scratch[0] if local else None
        self.sent = scratch[0]
        (
            self.pair, self.passing, self.r1, self.s2, self.r2, self.kept,
            self.csem, self.msem, self.nsem,
        ) = scratch[1:]
        self.b, self.y, self.x, self.k = place()

    def device(self, ax, d):
        y, x = self.y, self.x
        if ax == 0:
            x = lax.rem(x + d, 4)
        else:
            y = lax.rem(y + d, 4)
        return (self.b, (y * 4 + x) * 2 + self.k)

    def chunk(self, ax, d, core):
        if self.give is not None:
            return self.give.at[ax, d]
        if ax == 0:
            return self.source[ax].at[:, lax.rem(self.x + d, 4), core]
        return self.source[ax].at[lax.rem(self.y + d, 4), :, core]

    def pair_copy(self, ax, d):
        return pltpu.make_async_remote_copy(
            src_ref=self.chunk(ax, d, 1 - self.k),
            dst_ref=self.pair.at[ax, d],
            send_sem=self.csem.at[ax, d, 1],
            recv_sem=self.csem.at[ax, d, 2],
            device_id=(self.b, (self.y * 4 + self.x) * 2 + 1 - self.k),
            device_id_type=MESH,
        )

    def begin(self):
        for d in ORDER:
            for ax in range(2):
                self.pair_copy(ax, d).start()

    def form(self, tables, e, slots, running):
        for h in range(4):
            running[h] = jnp.zeros((QUARTER, LEAF), F32)

        @pl.loop(0, CAP // GROUP)
        def _(g):
            terms = [contribution(slots[tables[FAR_ORDER + e * CAP + g * GROUP + i]]) for i in range(GROUP)]
            for h in range(4):
                total = running[4 * GROUP * g + h]
                for i in range(GROUP):
                    s = g * GROUP + i
                    here = tables[FAR_TARGET + e * CAP + s]
                    same = (here == tables[FAR_TARGET + e * CAP + s - 1]).astype(jnp.int32)
                    total = total * same.astype(F32) + terms[i][h * QUARTER : (h + 1) * QUARTER]
                    running[4 * (s + 1) + h] = total

        for d in ORDER:
            for ax in range(2):

                @pl.loop(0, 4)
                def _(q):
                    place = (q * 4 + lax.rem(self.x + d, 4)) if ax == 0 else (lax.rem(self.y + d, 4) * 4 + q)
                    first = FAR_LAST + e * TARGETS + place * 2
                    for ref, core in ((self.give, 1 - self.k), (self.own, self.k)):
                        spot = 4 * tables[first + core] + 2 * ax
                        for h in range(2):
                            ref[ax, d, q, h * QUARTER : (h + 1) * QUARTER, :] = running[spot + h].astype(BF16)

                self.pair_copy(ax, d).start()

    def arrived(self, ax, d):
        self.pair_copy(ax, d).wait_recv()

    def gave(self):
        if not self.given:
            for d in ORDER:
                for ax in range(2):
                    self.pair_copy(ax, d).wait_send()
        self.given = True

    def out(self, ax, d):
        return self.sent.at[ax, d if self.own is not None else d - 1]

    def mine(self, ax, d, q):
        if self.own is not None:
            value = self.own[ax, d, q]
        elif ax == 0:
            value = self.source[ax][q, lax.rem(self.x + d, 4), self.k]
        else:
            value = self.source[ax][lax.rem(self.y + d, 4), q, self.k]
        return value.astype(F32) + self.pair[ax, d, q].astype(F32)

    def ring_copy(self, ax, side, part):
        low = 2 * side if part == 0 else 2 * side if part == 2 else 2 - 2 * side
        rows = pl.ds(low, 2)
        return pltpu.make_async_remote_copy(
            src_ref=self.out(ax, 2 if part == 0 else SIDES[side]).at[rows],
            dst_ref=self.passing.at[ax, side] if part == 0 else self.r1.at[ax, side, rows],
            send_sem=self.msem.at[ax, side, part, 0],
            recv_sem=self.msem.at[ax, side, part, 1],
            device_id=self.device(ax, SIDES[side]),
            device_id_type=MESH,
        )

    def last_copy(self, ax, d):
        return pltpu.make_async_remote_copy(
            src_ref=self.s2.at[ax, d - 1],
            dst_ref=self.r2.at[ax, d - 1],
            send_sem=self.nsem.at[ax, d - 1, 0],
            recv_sem=self.nsem.at[ax, d - 1, 1],
            device_id=self.device(1 - ax, d),
            device_id_type=MESH,
        )

    def opposite(self):
        for ax in range(2):
            self.arrived(ax, 2)
            for side in range(2):

                @pl.loop(2 * side, 2 * side + 2)
                def _(q):
                    self.out(ax, 2)[q] = self.mine(ax, 2, q).astype(BF16)

                self.ring_copy(ax, side, 0).start()

    def beside(self):
        for side in range(2):
            for ax in range(2):
                self.arrived(ax, SIDES[side])

                @pl.loop(2 - 2 * side, 4 - 2 * side)
                def _(q):
                    self.out(ax, SIDES[side])[q] = self.mine(ax, SIDES[side], q).astype(BF16)

                self.ring_copy(ax, side, 1).start()

    def relay(self):
        for ax in range(2):
            for side in range(2):
                self.ring_copy(ax, side, 0).wait_recv()

                @pl.loop(0, 2)
                def _(p):
                    q = 2 * side + p
                    total = self.mine(ax, SIDES[side], q) + self.passing[ax, side, p].astype(F32)
                    self.out(ax, SIDES[side])[q] = total.astype(BF16)

                self.ring_copy(ax, side, 2).start()

    def turn(self):
        for ax in range(2):
            self.arrived(ax, 0)
        for ax in range(2):
            for part in (1, 2):
                for side in range(2):
                    self.ring_copy(ax, side, part).wait_recv()
            here = self.y if ax == 0 else self.x
            for d in ORDER:
                q = lax.rem(here + d, 4)
                total = self.mine(ax, 0, q)
                for side in range(2):
                    total = total + self.r1[ax, side, q].astype(F32)
                if d == 0:
                    self.kept[ax] = total
                else:
                    self.s2[ax, d - 1] = total.astype(BF16)
                    self.last_copy(ax, d).start()

    def total(self, ax):
        for d in (1, 3, 2):
            self.last_copy(ax, d).wait_recv()
        total = self.kept[ax]
        for p in range(3):
            total = total + self.r2[ax, p].astype(F32)
        return total

    def finish(self):
        self.gave()
        for ax in range(2):
            for side in range(2):
                for part in range(3):
                    self.ring_copy(ax, side, part).wait_send()
            for d in range(1, 4):
                self.last_copy(ax, d).wait_send()

    def partners(self):
        near = [self.device(ax, d) for ax in range(2) for d in range(1, 4)]
        return near + [(self.b, (self.y * 4 + self.x) * 2 + 1 - self.k)]


def greet(partners):
    barrier = pltpu.get_barrier_semaphore()
    for partner in partners:
        pl.semaphore_signal(barrier, inc=1, device_id=partner, device_id_type=MESH)
    pl.semaphore_wait(barrier, len(partners))


def exchange_kernel(slots, tables_in, loads, dense, received, results, sums0, sums1, *scratch):
    sums = (sums0, sums1)
    gives = scratch[30:32]
    planes = [PlaneSum(None, scratch[10 * e : 10 * e + 10], gives[e % 2]) for e in range(len(FAR))]
    far_slots = scratch[32:35]
    tables, turned, blocks, running, zsem, lsem, dsem = scratch[35:]
    b = lax.axis_index("blk")
    c = lax.axis_index("col")

    def above(d):
        return (lax.rem(b + d, PLANES), c)

    own_slots = pltpu.make_async_copy(slots.at[0], received.at[pl.ds(len(NEAR) * CAP, CAP)], lsem.at[0])
    table_copy = pltpu.make_async_copy(tables_in, tables, lsem.at[1])
    far_copies = [
        pltpu.make_async_copy(slots.at[d], far_slots[e], lsem.at[2 + e]) for e, d in enumerate(FAR)
    ]
    part = DENSE // PIECES
    dense_copies = [
        pltpu.make_async_copy(dense.at[pl.ds(p * part, part)], blocks.at[pl.ds(p * part, part)], dsem.at[p])
        for p in range(PIECES)
    ]
    for copy in [table_copy] + far_copies:
        copy.start()
    greet(planes[0].partners() + [above(d) for d in NEAR])
    moves = [
        pltpu.make_async_remote_copy(
            src_ref=slots.at[d],
            dst_ref=received.at[pl.ds(i * CAP, CAP)],
            send_sem=zsem.at[i, 0],
            recv_sem=zsem.at[i, 1],
            device_id=above(d),
            device_id_type=MESH,
        )
        for i, d in enumerate(NEAR)
    ]
    for move in moves:
        move.start()
    for copy in [own_slots] + dense_copies:
        copy.start()
    received[NULL] = jnp.zeros((2 * RANK, LEAF), BF16)

    def dense_sums(part):
        low = part * QUARTER
        running[0] = jnp.zeros((QUARTER, LEAF), F32)

        @pl.loop(0, DENSE // GROUP)
        def _(g):
            terms = [
                jnp.dot(
                    turned[tables[SOURCED + g * GROUP + i], low : low + QUARTER, :],
                    blocks[tables[ORDERED + g * GROUP + i]],
                    preferred_element_type=F32,
                )
                for i in range(GROUP)
            ]
            total = running[g * GROUP]
            for i in range(GROUP):
                here = tables[TARGETED + g * GROUP + i]
                same = (here == tables[TARGETED + g * GROUP + i - 1]).astype(jnp.int32)
                total = total * same.astype(F32) + terms[i]
                running[g * GROUP + i + 1] = total

        @pl.loop(0, TARGETS)
        def _(t):
            sums[low // HALF][t, low % HALF : low % HALF + QUARTER, :] = running[tables[LAST + t]] * tables[HAS + t].astype(F32)


    table_copy.wait()
    for e, plane in enumerate(planes):
        far_copies[e].wait()
        if e == 2:
            planes[0].gave()
        plane.form(tables, e, far_slots[e], running)
        plane.opposite()
        plane.beside()
        if e == 1:
            planes[0].relay()
    for s in range(SOURCES):
        turned[s] = loads[s].T
    planes[1].relay()
    for copy in dense_copies:
        copy.wait()
    dense_sums(0)
    dense_sums(1)
    planes[0].turn()
    planes[2].relay()
    dense_sums(2)
    dense_sums(3)
    planes[1].turn()
    planes[2].turn()
    for e, plane in enumerate(planes):
        for ax in range(2):
            results[e, ax * HALF : (ax + 1) * HALF, :] = plane.total(ax).astype(BF16)
    for plane in planes:
        plane.finish()
    own_slots.wait()
    for move in moves:
        move.wait()


def exchange(slots, tables, loads, dense):
    scratch = []
    for _ in FAR:
        scratch += reduce_scratch(BF16, True)
    return pl.pallas_call(
        exchange_kernel,
        out_shape=(
            jax.ShapeDtypeStruct((NULL + 1, 2 * RANK, LEAF), BF16),
            jax.ShapeDtypeStruct((len(FAR), CASES, LEAF), BF16),
            jax.ShapeDtypeStruct((TARGETS, HALF, LEAF), F32),
            jax.ShapeDtypeStruct((TARGETS, HALF, LEAF), F32),
        ),
        in_specs=[spec(pl.ANY), spec(pl.ANY), spec(pltpu.VMEM), spec(pl.ANY)],
        out_specs=(spec(pltpu.VMEM),) * 4,
        scratch_shapes=scratch
        + [pltpu.VMEM((2, 4, 4, HALF, LEAF), BF16)] * 2
        + [pltpu.VMEM((CAP, 2 * RANK, LEAF), BF16)] * len(FAR)
        + [
            pltpu.SMEM((TABLE,), jnp.int32),
            pltpu.VMEM((SOURCES, CASES, LEAF), BF16),
            pltpu.VMEM((DENSE, LEAF, LEAF), BF16),
            pltpu.VMEM((4 * (CAP + 1), QUARTER, LEAF), F32),
            pltpu.SemaphoreType.DMA((len(NEAR), 2)),
            pltpu.SemaphoreType.DMA((5,)),
            pltpu.SemaphoreType.DMA((PIECES,)),
        ],
        compiler_params=pltpu.CompilerParams(
            collective_id=1, has_side_effects=True, vmem_limit_bytes=40 * MIB
        ),
        name="exchange",
    )(slots, tables, loads, dense)


def gather_kernel(tables, received, in0, in1, sums0, sums1):
    @pl.loop(0, lax.div(tables[LENGTH] + NEAR_GROUP - 1, NEAR_GROUP))
    def _(g):
        terms = [contribution(received[tables[SPOTS + g * NEAR_GROUP + i]]) for i in range(NEAR_GROUP)]
        for i in range(NEAR_GROUP):
            t = tables[IDS + g * NEAR_GROUP + i]
            sums0[t] += terms[i][:HALF]
            sums1[t] += terms[i][HALF:]


def gather(tables, received, sums):
    return pl.pallas_call(
        gather_kernel,
        out_shape=(jax.ShapeDtypeStruct((TARGETS, HALF, LEAF), F32),) * 2,
        in_specs=[spec(pltpu.SMEM)] + [spec(pltpu.VMEM)] * 3,
        out_specs=(spec(pltpu.VMEM),) * 2,
        input_output_aliases={2: 0, 3: 1},
        compiler_params=pltpu.CompilerParams(vmem_limit_bytes=8 * MIB),
        name="gather",
    )(tables, received, *sums)


def final_kernel(source0, source1, results, out, *scratch):
    own = PlaneSum((source0, source1), scratch[:10], None)
    landed, zsem = scratch[10:]
    b = lax.axis_index("blk")
    c = lax.axis_index("col")

    def above(d):
        return (lax.rem(b + d, PLANES), c)

    greet(own.partners() + [above(d) for d in FAR])
    moves = [
        pltpu.make_async_remote_copy(
            src_ref=results.at[e],
            dst_ref=landed.at[e],
            send_sem=zsem.at[e, 0],
            recv_sem=zsem.at[e, 1],
            device_id=above(d),
            device_id_type=MESH,
        )
        for e, d in enumerate(FAR)
    ]
    own.begin()
    for move in moves:
        move.start()
    own.opposite()
    own.beside()
    own.relay()
    own.turn()
    for move in moves:
        move.wait()
    for ax in range(2):
        total = own.total(ax)
        for e in range(len(FAR)):
            total = total + landed[e, ax * HALF : (ax + 1) * HALF, :].astype(F32)
        out[:, ax * HALF : (ax + 1) * HALF] = total.T.astype(BF16)
    own.finish()


def final(sums, results):
    return pl.pallas_call(
        final_kernel,
        out_shape=jax.ShapeDtypeStruct((LEAF, CASES), BF16),
        in_specs=[spec(pltpu.VMEM)] * 3,
        out_specs=spec(pltpu.VMEM),
        scratch_shapes=reduce_scratch(F32, False)
        + [pltpu.VMEM((len(FAR), CASES, LEAF), BF16), pltpu.SemaphoreType.DMA((len(FAR), 2))],
        compiler_params=pltpu.CompilerParams(
            collective_id=2, has_side_effects=True, vmem_limit_bytes=16 * MIB
        ),
        name="final",
    )(*[x.reshape(4, 4, 2, HALF, LEAF) for x in sums], results)


def shards(
    loads,
    dense_blocks,
    dense_source,
    dense_target,
    left_factors,
    right_factors,
    block_owner,
    block_source,
    block_target,
):
    loads = loads.reshape(SOURCES, LEAF, CASES)
    owner = block_owner.reshape(PLANES, LOW)
    source = block_source.reshape(PLANES, LOW)
    target = block_target.reshape(PLANES, LOW)
    left = left_factors.reshape(LOW, RANK, LEAF)
    right = right_factors.reshape(LOW, RANK, LEAF)
    slots, tables = pack(
        owner, source, target, dense_source.reshape(DENSE), dense_target.reshape(DENSE), loads, left, right
    )
    received, results, *sums = exchange(slots, tables, loads, dense_blocks.reshape(DENSE, LEAF, LEAF))
    sums = gather(tables, received, sums)
    return final(sums, results)


def solution(mesh):
    placed = (
        P("col", None),
        P("blk", "col", None, None, None),
        P("blk", "col", None),
        P("blk", "col", None),
        P("blk", "col", None, None, None),
        P("blk", "col", None, None, None),
        P(None, "col", None, None),
        P(None, "col", None),
        P(None, "col", None),
    )
    return jax.shard_map(
        shards, mesh=mesh, in_specs=placed, out_specs=P(("blk", "col"), None), check_vma=False
    )
```

```python
import jax
import jax.numpy as jnp
from jax import lax
from jax.experimental import pallas as pl
from jax.experimental.pallas import tpu as pltpu
from jax.sharding import PartitionSpec as P

LEAF = 256
HALF = 128
QUARTER = 64
CASES = 256
RANK = 32
SOURCES = 8
TARGETS = 32
DENSE = 60
LOW = 64
CAP = 16
PLANES = 8
GROUP = 4
NEAR_GROUP = 8
PIECES = 4
ORDERED = 0
SOURCED = 64
TARGETED = 128
LAST = 256
HAS = 288
IDS = 320
SPOTS = 416
LENGTH = 508
FAR_ORDER = 512
FAR_TARGET = 560
FAR_LAST = 608
TABLE = 768
NULL = 80
NEAR = (1, 7, 2, 6)
FAR = (4, 3, 5)
MESH = pl.DeviceIdType.MESH
MIB = 1 << 20
BF16 = jnp.bfloat16
F32 = jnp.float32


def spec(space):
    return pl.BlockSpec(memory_space=space)


def place():
    b = lax.axis_index("blk")
    c = lax.axis_index("col")
    return b, lax.div(c, 8), lax.rem(lax.div(c, 2), 4), lax.rem(c, 2)


def contribution(pair):
    return lax.dot_general(
        pair[RANK:], pair[:RANK], (((0,), (0,)), ((), ())), preferred_element_type=F32
    )


def pack_kernel(
    owner_in, source_in, target_in, dsource_in, dtarget_in, loads_in, left_in, right_in, slots_out, tables,
    owner, source, target, dsource, dtarget, loads, left, right, slots, count, where, tsem, vsem,
):
    b = lax.axis_index("blk")
    small = [
        pltpu.make_async_copy(x, y, tsem.at[i])
        for i, (x, y) in enumerate(
            (
                (owner_in, owner),
                (source_in, source),
                (target_in, target),
                (dsource_in, dsource),
                (dtarget_in, dtarget),
            )
        )
    ]
    large = [
        pltpu.make_async_copy(x, y, vsem.at[i])
        for i, (x, y) in enumerate(((loads_in, loads), (left_in, left), (right_in, right)))
    ]
    for copy in small + large:
        copy.start()
    for d in range(PLANES):
        count[d] = 0
    for t in range(TARGETS):
        tables[HAS + t] = 0
        tables[LAST + t] = 0

    def clear(i, carry):
        tables[FAR_LAST + i] = 0
        return carry

    lax.fori_loop(0, len(FAR) * TARGETS, clear, 0, unroll=16)

    def blank(i, carry):
        tables[FAR_ORDER + i] = 0
        tables[FAR_TARGET + i] = 0
        return carry

    lax.fori_loop(0, len(FAR) * CAP, blank, 0, unroll=16)
    for copy in small:
        copy.wait()

    def tally(n, carry):
        t = dtarget[n]
        tables[HAS + t] = tables[HAS + t] + 1
        return carry

    lax.fori_loop(0, DENSE, tally, 0, unroll=4)
    start = jnp.int32(0)
    for t in range(TARGETS):
        tables[LAST + t] = start
        start = start + tables[HAS + t]

    def sort(n, carry):
        t = dtarget[n]
        spot = tables[LAST + t]
        tables[LAST + t] = spot + 1
        tables[ORDERED + spot] = n
        tables[SOURCED + spot] = dsource[n]
        tables[TARGETED + spot] = t
        return carry

    lax.fori_loop(0, DENSE, sort, 0, unroll=4)
    for t in range(TARGETS):
        tables[HAS + t] = jnp.minimum(tables[HAS + t], 1)

    for copy in large:
        copy.wait()

    senders = [lax.rem(b - d + PLANES, PLANES) for d in NEAR + (0,)]

    def one(n, carry):
        d = lax.rem(owner[b, n] - b + PLANES, PLANES)
        r = count[d]
        count[d] = r + 1
        where[d * CAP + r] = target[b, n]
        coefficients = jnp.dot(left[n], loads[source[b, n]], preferred_element_type=F32)
        slots[d, r, :RANK, :] = right[n]
        slots[d, r, RANK:, :] = coefficients.astype(BF16)
        length, *ranks = carry
        for i, sender in enumerate(senders):
            tables[IDS + length] = target[sender, n]
            tables[SPOTS + length] = i * CAP + ranks[i]
            step = (owner[sender, n] == b).astype(jnp.int32)
            length = length + step
            ranks[i] = ranks[i] + step
        return (length, *ranks)

    length, *_ = lax.fori_loop(0, LOW, one, (jnp.int32(0),) * (2 + len(NEAR)), unroll=8)
    for j in range(NEAR_GROUP):
        tables[IDS + length + j] = 0
        tables[SPOTS + length + j] = NULL
    tables[LENGTH] = length
    whole = pltpu.make_async_copy(slots, slots_out, vsem.at[0])
    whole.start()

    for e, d in enumerate(FAR):
        amount = count[d]

        def add(r, carry, e=e, d=d):
            t = where[d * CAP + r]
            tables[FAR_LAST + e * TARGETS + t] = tables[FAR_LAST + e * TARGETS + t] + 1
            return carry

        lax.fori_loop(0, amount, add, 0)

        def begin(t, start, e=e):
            held = tables[FAR_LAST + e * TARGETS + t]
            tables[FAR_LAST + e * TARGETS + t] = start
            return start + held

        lax.fori_loop(0, TARGETS, begin, jnp.int32(0), unroll=8)

        def put(r, carry, e=e, d=d):
            t = where[d * CAP + r]
            spot = tables[FAR_LAST + e * TARGETS + t]
            tables[FAR_LAST + e * TARGETS + t] = spot + 1
            tables[FAR_ORDER + e * CAP + spot] = r
            tables[FAR_TARGET + e * CAP + spot] = t
            return carry

        lax.fori_loop(0, amount, put, 0)

        def last(t, before, e=e):
            end = tables[FAR_LAST + e * TARGETS + t]
            tables[FAR_LAST + e * TARGETS + t] = jnp.where(end == before, 0, end)
            return end

        lax.fori_loop(0, TARGETS, last, jnp.int32(0), unroll=8)

    whole.wait()


def pack(owner, source, target, dsource, dtarget, loads, left, right):
    return pl.pallas_call(
        pack_kernel,
        out_shape=(
            jax.ShapeDtypeStruct((PLANES, CAP, 2 * RANK, LEAF), BF16),
            jax.ShapeDtypeStruct((TABLE,), jnp.int32),
        ),
        in_specs=[spec(pl.ANY)] * 8,
        out_specs=(spec(pl.ANY), spec(pltpu.SMEM)),
        scratch_shapes=[
            pltpu.SMEM((PLANES, LOW), jnp.int32),
            pltpu.SMEM((PLANES, LOW), jnp.int32),
            pltpu.SMEM((PLANES, LOW), jnp.int32),
            pltpu.SMEM((DENSE,), jnp.int32),
            pltpu.SMEM((DENSE,), jnp.int32),
            pltpu.VMEM((SOURCES, LEAF, CASES), BF16),
            pltpu.VMEM((LOW, RANK, LEAF), BF16),
            pltpu.VMEM((LOW, RANK, LEAF), BF16),
            pltpu.VMEM((PLANES, CAP, 2 * RANK, LEAF), BF16),
            pltpu.SMEM((PLANES,), jnp.int32),
            pltpu.SMEM((PLANES * CAP,), jnp.int32),
            pltpu.SemaphoreType.DMA((5,)),
            pltpu.SemaphoreType.DMA((3,)),
        ],
        compiler_params=pltpu.CompilerParams(vmem_limit_bytes=60 * MIB),
        name="pack",
    )(owner, source, target, dsource, dtarget, loads, left, right)


def reduce_scratch(dtype, local):
    return [pltpu.VMEM((2, 4 if local else 3, 4, HALF, LEAF), BF16)] + [
        pltpu.VMEM((2, 4, 4, HALF, LEAF), dtype),
        pltpu.VMEM((2, 2, 2, HALF, LEAF), BF16),
        pltpu.VMEM((2, 2, 4, HALF, LEAF), BF16),
        pltpu.VMEM((2, 3, HALF, LEAF), BF16),
        pltpu.VMEM((2, 3, HALF, LEAF), BF16),
        pltpu.VMEM((2, HALF, LEAF), F32),
        pltpu.SemaphoreType.DMA((2, 4, 3)),
        pltpu.SemaphoreType.DMA((2, 2, 3, 2)),
        pltpu.SemaphoreType.DMA((2, 3, 2)),
    ]


ORDER = (2, 1, 3, 0)
SIDES = (1, 3)


class PlaneSum:
    def __init__(self, source, scratch, give):
        local = give is not None
        self.source = source
        self.give = give
        self.given = False
        self.own = scratch[0] if local else None
        self.sent = scratch[0]
        (
            self.pair, self.passing, self.r1, self.s2, self.r2, self.kept,
            self.csem, self.msem, self.nsem,
        ) = scratch[1:]
        self.b, self.y, self.x, self.k = place()

    def device(self, ax, d):
        y, x = self.y, self.x
        if ax == 0:
            x = lax.rem(x + d, 4)
        else:
            y = lax.rem(y + d, 4)
        return (self.b, (y * 4 + x) * 2 + self.k)

    def chunk(self, ax, d, core):
        if self.give is not None:
            return self.give.at[ax, d]
        if ax == 0:
            return self.source[ax].at[:, lax.rem(self.x + d, 4), core]
        return self.source[ax].at[lax.rem(self.y + d, 4), :, core]

    def pair_copy(self, ax, d):
        return pltpu.make_async_remote_copy(
            src_ref=self.chunk(ax, d, 1 - self.k),
            dst_ref=self.pair.at[ax, d],
            send_sem=self.csem.at[ax, d, 1],
            recv_sem=self.csem.at[ax, d, 2],
            device_id=(self.b, (self.y * 4 + self.x) * 2 + 1 - self.k),
            device_id_type=MESH,
        )

    def begin(self):
        for d in ORDER:
            for ax in range(2):
                self.pair_copy(ax, d).start()

    def form(self, tables, e, slots, running):
        for h in range(4):
            running[h] = jnp.zeros((QUARTER, LEAF), F32)

        @pl.loop(0, CAP // NEAR_GROUP)
        def _(g):
            terms = [contribution(slots[tables[FAR_ORDER + e * CAP + g * NEAR_GROUP + i]]) for i in range(NEAR_GROUP)]
            for h in range(4):
                total = running[4 * NEAR_GROUP * g + h]
                for i in range(NEAR_GROUP):
                    s = g * NEAR_GROUP + i
                    here = tables[FAR_TARGET + e * CAP + s]
                    same = (here == tables[FAR_TARGET + e * CAP + s - 1]).astype(jnp.int32)
                    total = total * same.astype(F32) + terms[i][h * QUARTER : (h + 1) * QUARTER]
                    running[4 * (s + 1) + h] = total

        for d in ORDER:
            for ax in range(2):

                @pl.loop(0, 4, unroll=4)
                def _(q):
                    place = (q * 4 + lax.rem(self.x + d, 4)) if ax == 0 else (lax.rem(self.y + d, 4) * 4 + q)
                    first = FAR_LAST + e * TARGETS + place * 2
                    for ref, core in ((self.give, 1 - self.k), (self.own, self.k)):
                        spot = 4 * tables[first + core] + 2 * ax
                        for h in range(2):
                            ref[ax, d, q, h * QUARTER : (h + 1) * QUARTER, :] = running[spot + h].astype(BF16)

                self.pair_copy(ax, d).start()

    def arrived(self, ax, d):
        self.pair_copy(ax, d).wait_recv()

    def gave(self):
        if not self.given:
            for d in ORDER:
                for ax in range(2):
                    self.pair_copy(ax, d).wait_send()
        self.given = True

    def out(self, ax, d):
        return self.sent.at[ax, d if self.own is not None else d - 1]

    def mine(self, ax, d, q):
        if self.own is not None:
            value = self.own[ax, d, q]
        elif ax == 0:
            value = self.source[ax][q, lax.rem(self.x + d, 4), self.k]
        else:
            value = self.source[ax][lax.rem(self.y + d, 4), q, self.k]
        return value.astype(F32) + self.pair[ax, d, q].astype(F32)

    def ring_copy(self, ax, side, part):
        low = 2 * side if part == 0 else 2 * side if part == 2 else 2 - 2 * side
        rows = pl.ds(low, 2)
        return pltpu.make_async_remote_copy(
            src_ref=self.out(ax, 2 if part == 0 else SIDES[side]).at[rows],
            dst_ref=self.passing.at[ax, side] if part == 0 else self.r1.at[ax, side, rows],
            send_sem=self.msem.at[ax, side, part, 0],
            recv_sem=self.msem.at[ax, side, part, 1],
            device_id=self.device(ax, SIDES[side]),
            device_id_type=MESH,
        )

    def last_copy(self, ax, d):
        return pltpu.make_async_remote_copy(
            src_ref=self.s2.at[ax, d - 1],
            dst_ref=self.r2.at[ax, d - 1],
            send_sem=self.nsem.at[ax, d - 1, 0],
            recv_sem=self.nsem.at[ax, d - 1, 1],
            device_id=self.device(1 - ax, d),
            device_id_type=MESH,
        )

    def opposite(self):
        for ax in range(2):
            self.arrived(ax, 2)
            for side in range(2):

                @pl.loop(2 * side, 2 * side + 2)
                def _(q):
                    self.out(ax, 2)[q] = self.mine(ax, 2, q).astype(BF16)

                self.ring_copy(ax, side, 0).start()

    def beside(self):
        for side in range(2):
            for ax in range(2):
                self.arrived(ax, SIDES[side])

                @pl.loop(2 - 2 * side, 4 - 2 * side)
                def _(q):
                    self.out(ax, SIDES[side])[q] = self.mine(ax, SIDES[side], q).astype(BF16)

                self.ring_copy(ax, side, 1).start()

    def relay(self):
        for ax in range(2):
            for side in range(2):
                self.ring_copy(ax, side, 0).wait_recv()

                @pl.loop(0, 2)
                def _(p):
                    q = 2 * side + p
                    total = self.mine(ax, SIDES[side], q) + self.passing[ax, side, p].astype(F32)
                    self.out(ax, SIDES[side])[q] = total.astype(BF16)

                self.ring_copy(ax, side, 2).start()

    def turn(self):
        for ax in range(2):
            self.arrived(ax, 0)
        for ax in range(2):
            for part in (1, 2):
                for side in range(2):
                    self.ring_copy(ax, side, part).wait_recv()
            here = self.y if ax == 0 else self.x
            for d in ORDER:
                q = lax.rem(here + d, 4)
                total = self.mine(ax, 0, q)
                for side in range(2):
                    total = total + self.r1[ax, side, q].astype(F32)
                if d == 0:
                    self.kept[ax] = total
                else:
                    self.s2[ax, d - 1] = total.astype(BF16)
                    self.last_copy(ax, d).start()

    def total(self, ax):
        for d in (1, 3, 2):
            self.last_copy(ax, d).wait_recv()
        total = self.kept[ax]
        for p in range(3):
            total = total + self.r2[ax, p].astype(F32)
        return total

    def finish(self):
        self.gave()
        for ax in range(2):
            for side in range(2):
                for part in range(3):
                    self.ring_copy(ax, side, part).wait_send()
            for d in range(1, 4):
                self.last_copy(ax, d).wait_send()

    def partners(self):
        near = [self.device(ax, d) for ax in range(2) for d in range(1, 4)]
        return near + [(self.b, (self.y * 4 + self.x) * 2 + 1 - self.k)]


def greet(partners):
    barrier = pltpu.get_barrier_semaphore()
    for partner in partners:
        pl.semaphore_signal(barrier, inc=1, device_id=partner, device_id_type=MESH)
    pl.semaphore_wait(barrier, len(partners))


def exchange_kernel(slots, tables_in, loads, dense, received, results, sums0, sums1, *scratch):
    sums = (sums0, sums1)
    gives = scratch[30:32]
    planes = [PlaneSum(None, scratch[10 * e : 10 * e + 10], gives[e % 2]) for e in range(len(FAR))]
    far_slots = scratch[32:35]
    tables, turned, blocks, running, zsem, lsem, dsem = scratch[35:]
    b = lax.axis_index("blk")
    c = lax.axis_index("col")

    def above(d):
        return (lax.rem(b + d, PLANES), c)

    own_slots = pltpu.make_async_copy(slots.at[0], received.at[pl.ds(len(NEAR) * CAP, CAP)], lsem.at[0])
    table_copy = pltpu.make_async_copy(tables_in, tables, lsem.at[1])
    far_copies = [
        pltpu.make_async_copy(slots.at[d], far_slots[e], lsem.at[2 + e]) for e, d in enumerate(FAR)
    ]
    part = DENSE // PIECES
    dense_copies = [
        pltpu.make_async_copy(dense.at[pl.ds(p * part, part)], blocks.at[pl.ds(p * part, part)], dsem.at[p])
        for p in range(PIECES)
    ]
    for copy in [table_copy] + far_copies:
        copy.start()
    greet(planes[0].partners() + [above(d) for d in NEAR])
    moves = [
        pltpu.make_async_remote_copy(
            src_ref=slots.at[d],
            dst_ref=received.at[pl.ds(i * CAP, CAP)],
            send_sem=zsem.at[i, 0],
            recv_sem=zsem.at[i, 1],
            device_id=above(d),
            device_id_type=MESH,
        )
        for i, d in enumerate(NEAR)
    ]
    for move in moves:
        move.start()
    for copy in [own_slots] + dense_copies:
        copy.start()
    received[NULL] = jnp.zeros((2 * RANK, LEAF), BF16)

    def dense_sums(part):
        low = part * QUARTER
        running[0] = jnp.zeros((QUARTER, LEAF), F32)

        @pl.loop(0, DENSE // GROUP)
        def _(g):
            terms = [
                jnp.dot(
                    turned[tables[SOURCED + g * GROUP + i], low : low + QUARTER, :],
                    blocks[tables[ORDERED + g * GROUP + i]],
                    preferred_element_type=F32,
                )
                for i in range(GROUP)
            ]
            total = running[g * GROUP]
            for i in range(GROUP):
                here = tables[TARGETED + g * GROUP + i]
                same = (here == tables[TARGETED + g * GROUP + i - 1]).astype(jnp.int32)
                total = total * same.astype(F32) + terms[i]
                running[g * GROUP + i + 1] = total

        @pl.loop(0, TARGETS)
        def _(t):
            sums[low // HALF][t, low % HALF : low % HALF + QUARTER, :] = running[tables[LAST + t]] * tables[HAS + t].astype(F32)


    table_copy.wait()
    for e, plane in enumerate(planes):
        far_copies[e].wait()
        if e == 2:
            planes[0].gave()
        plane.form(tables, e, far_slots[e], running)
        plane.opposite()
        plane.beside()
        if e == 1:
            planes[0].relay()
    for s in range(SOURCES):
        turned[s] = loads[s].T
    planes[1].relay()
    for copy in dense_copies:
        copy.wait()
    dense_sums(0)
    dense_sums(1)
    planes[0].turn()
    planes[2].relay()
    dense_sums(2)
    dense_sums(3)
    planes[1].turn()
    planes[2].turn()
    for e, plane in enumerate(planes):
        for ax in range(2):
            results[e, ax * HALF : (ax + 1) * HALF, :] = plane.total(ax).astype(BF16)
    for plane in planes:
        plane.finish()
    own_slots.wait()
    for move in moves:
        move.wait()


def exchange(slots, tables, loads, dense):
    scratch = []
    for _ in FAR:
        scratch += reduce_scratch(BF16, True)
    return pl.pallas_call(
        exchange_kernel,
        out_shape=(
            jax.ShapeDtypeStruct((NULL + 1, 2 * RANK, LEAF), BF16),
            jax.ShapeDtypeStruct((len(FAR), CASES, LEAF), BF16),
            jax.ShapeDtypeStruct((TARGETS, HALF, LEAF), F32),
            jax.ShapeDtypeStruct((TARGETS, HALF, LEAF), F32),
        ),
        in_specs=[spec(pl.ANY), spec(pl.ANY), spec(pltpu.VMEM), spec(pl.ANY)],
        out_specs=(spec(pltpu.VMEM),) * 4,
        scratch_shapes=scratch
        + [pltpu.VMEM((2, 4, 4, HALF, LEAF), BF16)] * 2
        + [pltpu.VMEM((CAP, 2 * RANK, LEAF), BF16)] * len(FAR)
        + [
            pltpu.SMEM((TABLE,), jnp.int32),
            pltpu.VMEM((SOURCES, CASES, LEAF), BF16),
            pltpu.VMEM((DENSE, LEAF, LEAF), BF16),
            pltpu.VMEM((4 * (CAP + 1), QUARTER, LEAF), F32),
            pltpu.SemaphoreType.DMA((len(NEAR), 2)),
            pltpu.SemaphoreType.DMA((5,)),
            pltpu.SemaphoreType.DMA((PIECES,)),
        ],
        compiler_params=pltpu.CompilerParams(
            collective_id=1, has_side_effects=True, vmem_limit_bytes=40 * MIB
        ),
        name="exchange",
    )(slots, tables, loads, dense)


def gather_kernel(tables, received, in0, in1, sums0, sums1):
    @pl.loop(0, lax.div(tables[LENGTH] + NEAR_GROUP - 1, NEAR_GROUP))
    def _(g):
        terms = [contribution(received[tables[SPOTS + g * NEAR_GROUP + i]]) for i in range(NEAR_GROUP)]
        for i in range(NEAR_GROUP):
            t = tables[IDS + g * NEAR_GROUP + i]
            sums0[t] += terms[i][:HALF]
            sums1[t] += terms[i][HALF:]


def gather(tables, received, sums):
    return pl.pallas_call(
        gather_kernel,
        out_shape=(jax.ShapeDtypeStruct((TARGETS, HALF, LEAF), F32),) * 2,
        in_specs=[spec(pltpu.SMEM)] + [spec(pltpu.VMEM)] * 3,
        out_specs=(spec(pltpu.VMEM),) * 2,
        input_output_aliases={2: 0, 3: 1},
        compiler_params=pltpu.CompilerParams(vmem_limit_bytes=8 * MIB),
        name="gather",
    )(tables, received, *sums)


def final_kernel(source0, source1, results, out, *scratch):
    own = PlaneSum((source0, source1), scratch[:10], None)
    landed, zsem = scratch[10:]
    b = lax.axis_index("blk")
    c = lax.axis_index("col")

    def above(d):
        return (lax.rem(b + d, PLANES), c)

    greet(own.partners() + [above(d) for d in FAR])
    moves = [
        pltpu.make_async_remote_copy(
            src_ref=results.at[e],
            dst_ref=landed.at[e],
            send_sem=zsem.at[e, 0],
            recv_sem=zsem.at[e, 1],
            device_id=above(d),
            device_id_type=MESH,
        )
        for e, d in enumerate(FAR)
    ]
    own.begin()
    for move in moves:
        move.start()
    own.opposite()
    own.beside()
    own.relay()
    own.turn()
    for move in moves:
        move.wait()
    for ax in range(2):
        total = own.total(ax)
        for e in range(len(FAR)):
            total = total + landed[e, ax * HALF : (ax + 1) * HALF, :].astype(F32)
        out[:, ax * HALF : (ax + 1) * HALF] = total.T.astype(BF16)
    own.finish()


def final(sums, results):
    return pl.pallas_call(
        final_kernel,
        out_shape=jax.ShapeDtypeStruct((LEAF, CASES), BF16),
        in_specs=[spec(pltpu.VMEM)] * 3,
        out_specs=spec(pltpu.VMEM),
        scratch_shapes=reduce_scratch(F32, False)
        + [pltpu.VMEM((len(FAR), CASES, LEAF), BF16), pltpu.SemaphoreType.DMA((len(FAR), 2))],
        compiler_params=pltpu.CompilerParams(
            collective_id=2, has_side_effects=True, vmem_limit_bytes=16 * MIB
        ),
        name="final",
    )(*[x.reshape(4, 4, 2, HALF, LEAF) for x in sums], results)


def shards(
    loads,
    dense_blocks,
    dense_source,
    dense_target,
    left_factors,
    right_factors,
    block_owner,
    block_source,
    block_target,
):
    loads = loads.reshape(SOURCES, LEAF, CASES)
    owner = block_owner.reshape(PLANES, LOW)
    source = block_source.reshape(PLANES, LOW)
    target = block_target.reshape(PLANES, LOW)
    left = left_factors.reshape(LOW, RANK, LEAF)
    right = right_factors.reshape(LOW, RANK, LEAF)
    slots, tables = pack(
        owner, source, target, dense_source.reshape(DENSE), dense_target.reshape(DENSE), loads, left, right
    )
    received, results, *sums = exchange(slots, tables, loads, dense_blocks.reshape(DENSE, LEAF, LEAF))
    sums = gather(tables, received, sums)
    return final(sums, results)


def solution(mesh):
    placed = (
        P("col", None),
        P("blk", "col", None, None, None),
        P("blk", "col", None),
        P("blk", "col", None),
        P("blk", "col", None, None, None),
        P("blk", "col", None, None, None),
        P(None, "col", None, None),
        P(None, "col", None),
        P(None, "col", None),
    )
    return jax.shard_map(
        shards, mesh=mesh, in_specs=placed, out_specs=P(("blk", "col"), None), check_vma=False
    )
```
